256 devices in a mesh: space: 32 (over z_lo, x, core), mode: 8 (over y, z_hi).
Axes of the slice: x: 4, y: 4, z: 8 (z_hi: 2, z_lo: 4; z = z_hi * 4 + z_lo), core: 2. Of those that a mesh axis runs over, the one named last changes fastest.
Arguments:
- pressure: float32 [56, 256, 32, 128], P('mode', 'space'), may hold values from -0.3 to 0.3
- source: float32 [56, 256, 32, 128], P('mode', 'space'), may hold values from -4 to 4
- kl_field: float32 [6, 256, 32, 128], P(None, 'space'), may hold values from -3 to 10, as said below
- coupling_list: int32 [4, 210], replicated, may hold values from 0 to 55, as said below
Outputs:
- correction: float32 [56, 256, 32, 128], P('mode', 'space')
- residual: float32 [56, 256, 32, 128], P('mode', 'space')
The draws below stay inside these ranges and needn't reach their ends.
Inputs may be any that keep to these rules, and one draw needn't show every extreme that they name: Column n states that mode coupling_list[0, n] couples to mode coupling_list[1, n] through field coupling_list[2, n], from 1 to 5, with the weight sqrt(coupling_list[3, n]), the code running from 1 to 3. The columns are all couplings of the normalized Hermite chaos of total degree 3 in 5 variables, each once, under a numbering of the 56 modes and an order of the columns drawn from the seed; with (i, j, k, code) the list also holds (j, i, k, code). kl_field[0], the mean permeability, lies between 1 and 10; the fields 1 to 5 lie between -3 and 3.
All inputs are finite; a program needn't handle non-finite values.
Results may differ from the reference program's by a relative error of at most 0.0003.
Values sent between devices are 32-bit elements; how exact they have to be, the bound alone decides.
A program may use at most 128 MiB of HBM per device.

```python
import math
import jax
import jax.numpy as jnp
import numpy as np
from jax import lax

P_SIZE = 56
KL = 5
DEG = 3
NNZ = 210
NY = 32
NZ = 128
SWEEPS = 2
COARSE = 8
LEVELS = 4
NX = 256


def multi_indices(count, degree):
    if count == 0:
        return [()]
    collected = []
    for leading in range(degree + 1):
        for remainder in multi_indices(count - 1, degree - leading):
            collected.append((leading,) + remainder)
    return collected


def chaos_pairs(count, degree):
    indices = multi_indices(count, degree)
    lookup = {entry: place for place, entry in enumerate(indices)}
    firsts, seconds, fields, codes = ([], [], [], [])
    for place, entry in enumerate(indices):
        if sum(entry) < degree:
            for axis in range(count):
                raised = list(entry)
                raised[axis] += 1
                other = lookup[tuple(raised)]
                firsts += [place, other]
                seconds += [other, place]
                fields += [axis + 1, axis + 1]
                codes += [raised[axis], raised[axis]]
    return np.array([firsts, seconds, fields, codes], dtype=np.int32)


def draw_coupling_list(key, part):
    key = jax.random.fold_in(key, 11)
    table = jnp.asarray(chaos_pairs(KL, DEG))
    labels = jax.random.permutation(jax.random.fold_in(key, 1), P_SIZE).astype(jnp.int32)
    order = jax.random.permutation(jax.random.fold_in(key, 2), NNZ)
    firsts = labels[table[0]][order]
    seconds = labels[table[1]][order]
    return jnp.stack([firsts, seconds, table[2][order], table[3][order]]).astype(jnp.int32)


def draw_kl_field(key, part):
    key = jax.random.fold_in(key, 23)
    mean_key = jax.random.fold_in(key, 1)
    spread_key = jax.random.fold_in(key, 2)
    shape = (KL, NX, NY, NZ)
    mean = jnp.exp(jax.random.uniform(mean_key, (1, NX, NY, NZ), jnp.float32, 0.0, math.log(10.0)))
    mean = jnp.clip(mean, 1.0, 10.0)
    spread = jax.random.truncated_normal(spread_key, -3.0, 3.0, shape, jnp.float32)
    return jnp.concatenate([mean, spread], axis=0).astype(jnp.float32)


def draw_source(key, part):
    key = jax.random.fold_in(key, 37)
    shape = (P_SIZE, NX, NY, NZ)
    return jax.random.truncated_normal(key, -4.0, 4.0, shape, jnp.float32)


def block_levels(key, dims, shards, least, top_value):
    level, own = 1.0, jax.random.fold_in(key, 6)
    for position, parts in shards:
        steps = jnp.exp(jax.random.uniform(jax.random.fold_in(own, position), (parts,), jnp.float32, least / len(shards), top_value / len(shards)))
        level = level * jnp.repeat(steps, dims[position] // parts).reshape([-1 if axis == position else 1 for axis in range(len(dims))])
    return level


def setup_inputs(seed: int = 0) -> dict:
    seeds = jax.random.split(jax.random.key(seed), 5)
    return {
        "pressure": jnp.clip(jax.random.uniform(seeds[0], (P_SIZE, NX, NY, NZ), jnp.float32, -0.3, 0.3) * block_levels(seeds[0], (P_SIZE, NX, NY, NZ), ((0, 8), (1, 32)), -0.4, 0.0), -0.3, 0.3),
        "source": draw_source(jax.random.fold_in(seeds[4], 71), 0),
        "kl_field": draw_kl_field(jax.random.fold_in(seeds[4], 71), 0),
        "coupling_list": draw_coupling_list(jax.random.fold_in(seeds[4], 71), 0),
    }


damping = 0.8

def shifted(values, axis, step):
    axis = axis % values.ndim
    size = values.shape[axis]
    widths = [(0, 0)] * values.ndim
    if step > 0:
        widths[axis] = (0, 1)
        return lax.slice_in_dim(jnp.pad(values, widths), 1, size + 1, axis=axis)
    widths[axis] = (1, 0)
    return lax.slice_in_dim(jnp.pad(values, widths), 0, size, axis=axis)

def faces_of(field):
    collected = []
    for axis in (-3, -2, -1):
        for step in (1, -1):
            face = 0.5 * (field + shifted(field, axis, step))
            if axis != -3:
                face = face * shifted(jnp.ones_like(field), axis, step)
            collected.append(face)
    return collected

def apply_operator(faces, values, scale):
    others = [shifted(values, axis, step) for axis in (-3, -2, -1) for step in (1, -1)]
    total = faces[0] * (values - others[0])
    for face, other in zip(faces[1:], others[1:]):
        total = total + face * (values - other)
    return scale * total

def diagonal_of(faces, scale):
    total = faces[0]
    for face in faces[1:]:
        total = total + face
    return scale * total

def restrict(values):
    cells = values[..., 0::2] + values[..., 1::2]
    cells = cells[..., 0::2, :] + cells[..., 1::2, :]
    cells = cells[..., 0::2, :, :] + cells[..., 1::2, :, :]
    return 0.125 * cells

def prolong(values):
    cells = jnp.repeat(values, 2, axis=-1)
    cells = jnp.repeat(cells, 2, axis=-2)
    return jnp.repeat(cells, 2, axis=-3)

def line_solve(faces, rest, scale):
    upper = scale * lax.optimization_barrier(jnp.sum(faces[0], axis=(-2, -1)))
    lower = scale * lax.optimization_barrier(jnp.sum(faces[1], axis=(-2, -1)))
    count = upper.shape[0]
    places = jnp.arange(count, dtype=jnp.int32)
    above = jnp.where(places < count - 1, -upper, jnp.zeros_like(upper))
    below = jnp.where(places > 0, -lower, jnp.zeros_like(lower))
    middle = upper + lower
    right = jnp.transpose(lax.optimization_barrier(jnp.sum(rest, axis=(-2, -1))))
    solved = lax.linalg.tridiagonal_solve(below, middle, above, right)
    return jnp.transpose(solved)[:, :, None, None]

def cycle(residual, field, level):
    scale = 0.25 ** level
    faces = faces_of(field)
    diagonal = diagonal_of(faces, scale)
    correction = damping * residual / diagonal

    def sweep(current):
        return current + damping * (residual - apply_operator(faces, current, scale)) / diagonal
    if level == LEVELS - 1:
        for turn in range(COARSE - 1):
            correction = sweep(correction)
        rest = residual - apply_operator(faces, correction, scale)
        return correction + line_solve(faces, rest, scale)
    for turn in range(SWEEPS - 1):
        correction = sweep(correction)
    rest = residual - apply_operator(faces, correction, scale)
    deeper = cycle(restrict(rest), restrict(field), level + 1)
    correction = correction + prolong(deeper)
    for turn in range(SWEEPS):
        correction = sweep(correction)
    return correction

def coupling_tables(coupling_list):
    modes = jnp.arange(P_SIZE, dtype=jnp.int32)
    orders = jnp.arange(1, KL + 1, dtype=jnp.int32)
    firsts = (coupling_list[0][:, None] == modes[None, :]).astype(jnp.float32)
    seconds = (coupling_list[1][:, None] == modes[None, :]).astype(jnp.float32)
    weights = jnp.sqrt(coupling_list[3].astype(jnp.float32))
    which = (coupling_list[2][:, None] == orders[None, :]).astype(jnp.float32) * weights[:, None]
    return jnp.einsum('nk,ni,nj->kij', which, firsts, seconds, precision=lax.Precision.HIGHEST)

def reference(pressure, source, kl_field, coupling_list):
    tables = coupling_tables(coupling_list)
    image = apply_operator(faces_of(kl_field[0]), pressure, 1.0)
    for order in range(KL):
        mixed = jnp.einsum('ij,jxyz->ixyz', tables[order], pressure, precision=lax.Precision.HIGHEST)
        image = image + apply_operator(faces_of(kl_field[order + 1]), mixed, 1.0)
    residual = source - image
    correction = cycle(residual, kl_field[0], 0)
    return (correction, residual)
```

```python
import jax
import jax.numpy as jnp
from jax import lax
from jax.sharding import PartitionSpec as P
from jax.experimental import pallas as pl
from jax.experimental.pallas import tpu as pltpu

MESH = pl.DeviceIdType.MESH
F32 = jnp.float32
P_SIZE = 56
KL = 5
SWEEPS = 2
COARSE = 8
LEVELS = 4
LANES = 128
ROW = 8
COLS = 4
PAD = 16


def split_dot(values, matrix):
    high = values.astype(jnp.bfloat16)
    low = (values - high.astype(F32)).astype(jnp.bfloat16)
    return jnp.dot(high, matrix, preferred_element_type=F32) + jnp.dot(
        low, matrix, preferred_element_type=F32
    )


def pairing():
    wide = lax.broadcasted_iota(jnp.int32, (2 * LANES, LANES), 0)
    narrow = lax.broadcasted_iota(jnp.int32, (2 * LANES, LANES), 1)
    return jnp.where(wide // 2 == narrow, 1.0, 0.0).astype(jnp.bfloat16)


def spreading():
    narrow = lax.broadcasted_iota(jnp.int32, (LANES, 2 * LANES), 0)
    wide = lax.broadcasted_iota(jnp.int32, (LANES, 2 * LANES), 1)
    return jnp.where(wide // 2 == narrow, 1.0, 0.0).astype(jnp.bfloat16)


def level_faces(coef, faces, weight, inverse, first, count, step, rows, depth, scale, origin, width):
    bits = rows.bit_length() - 1
    lane = lax.broadcasted_iota(jnp.int32, (step, LANES), 1) & (depth - 1)
    place = lax.broadcasted_iota(jnp.int32, (step, LANES), 0)

    @pl.loop(0, count // step)
    def _(turn):
        base = pl.multiple_of(first + turn * step, 8)
        at = place + (base - PAD)
        y = at & (rows - 1)
        x = (at >> bits) + origin
        inside = jnp.logical_and(x >= 0, x < width)
        c = coef[pl.ds(base, step), :]
        others = (
            (coef[pl.ds(base + rows, step), :], None),
            (coef[pl.ds(base - rows, step), :], None),
            (coef[pl.ds(base + 1, step), :], y < rows - 1),
            (coef[pl.ds(base - 1, step), :], y > 0),
            (pltpu.roll(c, LANES - 1, 1), lane < depth - 1),
            (pltpu.roll(c, 1, 1), lane > 0),
        )
        sides = []
        total = jnp.zeros_like(c)
        for other, keep in others:
            face = 0.5 * (c + other)
            if keep is not None:
                face = jnp.where(keep, face, 0.0)
            sides.append(face)
            total = total + face
        part = jnp.where(inside, 0.8 / jnp.where(inside, total, 1.0), 0.0)
        weight[pl.ds(base, step), :] = part * (1.0 / scale)
        inverse[pl.ds(base, step), :] = jnp.where(inside, total * (scale * 1.25), 0.0)
        for n in range(6):
            faces[n, pl.ds(base, step), :] = part * sides[n]


def first_sweep(start, right, weight, modes, first, count, step):
    @pl.loop(0, count // step)
    def _(turn):
        base = pl.multiple_of(first + turn * step, 8)
        w = weight[pl.ds(base, step), :]
        for m in range(modes):
            start[m, pl.ds(base, step), :] = w * right[m, pl.ds(base, step), :]


def sweep(out, now, start, faces, modes, first, count, step, rows, keep=0.2, inverse=None):
    @pl.loop(0, count // step)
    def _(turn):
        base = pl.multiple_of(first + turn * step, 8)
        g = [faces[n, pl.ds(base, step), :] for n in range(6)]
        for m in range(modes):
            c = now[m, pl.ds(base, step), :]
            total = start[m, pl.ds(base, step), :] + (keep if inverse is None else -0.8) * c
            total = total + g[0] * now[m, pl.ds(base + rows, step), :]
            total = total + g[1] * now[m, pl.ds(base - rows, step), :]
            total = total + g[2] * now[m, pl.ds(base + 1, step), :]
            total = total + g[3] * now[m, pl.ds(base - 1, step), :]
            total = total + g[4] * pltpu.roll(c, LANES - 1, 1)
            total = total + g[5] * pltpu.roll(c, 1, 1)
            if inverse is not None:
                total = total * inverse[pl.ds(base, step), :]
            out[m, pl.ds(base, step), :] = total


def pair_xy(values, first, planes, rows, temp):
    for x in range(planes // 2):
        temp[pl.ds(x * rows, rows), :] = (
            values[pl.ds(first + 2 * x * rows, rows), :]
            + values[pl.ds(first + (2 * x + 1) * rows, rows), :]
        )
    half = planes // 2 * rows // 2
    return temp[pl.ds(0, half, 2), :] + temp[pl.ds(1, half, 2), :]


def restrict_pair(left, right, matrix):
    return 0.125 * split_dot(jnp.concatenate([left, right], axis=-1), matrix)


def prolong(fine, modes, fine_first, coarse, coarse_first, planes, rows, matrix, temp):
    count = planes * rows
    for p in range((modes + 1) // 2):
        both = split_dot(coarse[p, pl.ds(coarse_first, count), :], matrix)
        for part in range(2):
            m = 2 * p + part
            if m >= modes:
                continue
            child = both[:, part * LANES : (part + 1) * LANES]
            temp[pl.ds(0, count, 2), :] = child
            temp[pl.ds(1, count, 2), :] = child
            for x in range(planes):
                child_plane = temp[pl.ds(2 * x * rows, 2 * rows), :]
                for side in range(2):
                    at = pl.ds(fine_first + (2 * x + side) * 2 * rows, 2 * rows)
                    fine[m, at, :] = fine[m, at, :] + child_plane


def zero_all(ref):
    ref[...] = jnp.zeros(ref.shape, ref.dtype)


def cycle_kernel(
    geometry, b_ref, field_ref, out_ref,
    c0, w0, i0, g0, b0, s0, a0, d0,
    c1, w1, i1, g1, b1, s1, a1, d1,
    c2, w2, i2, g2, b2, s2, a2, d2,
    c3, w3, i3, g3, b3, s3, a3, d3,
    temp, line, sums, send_sem, recv_sem,
):
    modes, width, rows, blocks = geometry
    grid = width * blocks
    me = lax.axis_index("space")
    mode = lax.axis_index("mode")
    r1, r2, r3 = rows // 2, rows // 4, rows // 8
    n1, n2 = width // 2, width // 4
    row_at, col_at = me % ROW, me // ROW
    cols = blocks // ROW
    counter = [0]

    def start_copy(src, dst, target, exists=None):
        number = counter[0]
        counter[0] += 1
        copy = pltpu.make_async_remote_copy(
            src_ref=src, dst_ref=dst, send_sem=send_sem.at[number], recv_sem=recv_sem.at[number],
            device_id=(target, mode), device_id_type=MESH,
        )
        if exists is None:
            copy.start()
        else:
            pl.when(exists)(copy.start)
        return copy

    def shift_exists(delta):
        return me + delta < blocks if delta > 0 else me + delta >= 0

    sends = []

    def to_neighbour(src, dst, delta):
        copy = start_copy(src, dst, me + delta, shift_exists(delta))
        sends.append((copy, shift_exists(delta)))
        return (copy, shift_exists(-delta))

    def arrived(pair):
        copy, exists = pair
        if exists is None:
            copy.wait_recv()
        else:
            pl.when(exists)(copy.wait_recv)

    def row_peer(q):
        return col_at * ROW + (row_at + q) % ROW

    def col_peer(q):
        return ((col_at + q) % cols) * ROW + row_at

    for ref in (c0, b0, s0, a0, d0, c1, b1, s1, a1, d1, c2, b2, s2, a2, d2, c3, b3, s3, a3, d3):
        zero_all(ref)

    barrier = pltpu.get_barrier_semaphore()
    expected = ROW - 1 + cols - 1
    for delta in (1, -1, 2, -2):
        @pl.when(shift_exists(delta))
        def _():
            pl.semaphore_signal(barrier, inc=1, device_id=(me + delta, mode), device_id_type=MESH)
        expected = expected + jnp.where(shift_exists(delta), 1, 0)
    for q in range(1, ROW):
        pl.semaphore_signal(barrier, inc=1, device_id=(row_peer(q), mode), device_id_type=MESH)
    for q in range(1, cols):
        pl.semaphore_signal(barrier, inc=1, device_id=(col_peer(q), mode), device_id_type=MESH)
    pl.semaphore_wait(barrier, expected)

    own0 = PAD + 4 * rows
    size0 = width * rows
    halos = []
    halos.append(to_neighbour(b_ref.at[:, pl.ds(size0 - 3 * rows, 3 * rows)], b0.at[pl.ds(0, modes), pl.ds(own0 - 3 * rows, 3 * rows)], 1))
    halos.append(to_neighbour(b_ref.at[:, pl.ds(0, 3 * rows)], b0.at[pl.ds(0, modes), pl.ds(own0 + size0, 3 * rows)], -1))
    c_halos = []
    c_halos.append(to_neighbour(field_ref.at[0, pl.ds(size0 - 4 * rows, 4 * rows)], c0.at[pl.ds(own0 - 4 * rows, 4 * rows)], 1))
    c_halos.append(to_neighbour(field_ref.at[0, pl.ds(0, 4 * rows)], c0.at[pl.ds(own0 + size0, 4 * rows)], -1))
    c0[pl.ds(own0, size0), :] = field_ref[0]
    for m in range(modes):
        b0[m, pl.ds(own0, size0), :] = b_ref[m]

    merge = pairing()
    spread = spreading()

    own1 = PAD + 5 * r1
    size1 = n1 * r1
    part = pair_xy(c0, own0, width, rows, temp)
    c1[pl.ds(own1, size1), :] = restrict_pair(part, part, merge)
    c1_halos = [
        to_neighbour(c1.at[pl.ds(own1, size1)], c1.at[pl.ds(own1 - size1, size1)], 1),
        to_neighbour(c1.at[pl.ds(own1, size1)], c1.at[pl.ds(own1 + size1, size1)], -1),
        to_neighbour(c1.at[pl.ds(own1 + size1 - r1, r1)], c1.at[pl.ds(own1 - size1 - r1, r1)], 2),
        to_neighbour(c1.at[pl.ds(own1, r1)], c1.at[pl.ds(own1 + 2 * size1, r1)], -2),
    ]
    size2 = n2 * r2
    own2 = pl.multiple_of(PAD + me * size2, 8)
    group2 = pl.multiple_of(PAD + col_at * (ROW * size2), 8)
    part = pair_xy(c1, own1, n1, r1, temp)
    c2[pl.ds(own2, size2), :] = restrict_pair(part, part, merge)
    c2_row = []
    for q in range(1, ROW):
        copy = start_copy(c2.at[pl.ds(own2, size2)], c2.at[pl.ds(own2, size2)], row_peer(q))
        sends.append((copy, None))
        c2_row.append((copy, None))

    for pair in c_halos:
        arrived(pair)
    level_faces(c0, g0, w0, i0, PAD + rows, (width + 6) * rows, 16, rows, LANES, 1.0, me * width - 4, grid)

    for pair in c2_row:
        arrived(pair)
    c2_col = []
    for q in range(1, cols):
        at = pl.ds(group2, ROW * size2)
        copy = start_copy(c2.at[at], c2.at[at], col_peer(q))
        sends.append((copy, None))
        c2_col.append((copy, None))
    for pair in c1_halos:
        arrived(pair)
    level_faces(c1, g1, w1, i1, PAD + r1, (n1 + 8) * r1, 16, r1, LANES // 2, 0.25, me * n1 - 5, grid // 2)
    for pair in c2_col:
        arrived(pair)
    all2 = blocks * size2
    level_faces(c2, g2, w2, i2, PAD, all2, 32, r2, LANES // 4, 0.0625, 0, grid // 4)
    part = pair_xy(c2, PAD, blocks * n2, r2, temp)
    all3 = all2 // 4
    c3[pl.ds(PAD, all3), :] = restrict_pair(part, part, merge)
    level_faces(c3, g3, w3, i3, PAD, all3, 32, r3, LANES // 8, 0.015625, 0, grid // 8)
    columns = grid // 8
    gather = jnp.where(
        lax.broadcasted_iota(jnp.int32, (columns, all3), 1) // r3
        == lax.broadcasted_iota(jnp.int32, (columns, all3), 0), 1.0, 0.0)
    within = jnp.where(
        lax.broadcasted_iota(jnp.int32, (LANES, LANES), 1) // (LANES // 8)
        == lax.broadcasted_iota(jnp.int32, (LANES, LANES), 0) // (LANES // 8), 1.0, 0.0)

    def column_sums(values):
        return jnp.dot(
            jnp.dot(gather, values, precision=lax.Precision.HIGHEST, preferred_element_type=F32),
            within, precision=lax.Precision.HIGHEST, preferred_element_type=F32)

    diag3 = i3[pl.ds(PAD, all3), :]
    line[0] = column_sums(g3[1, pl.ds(PAD, all3), :] * diag3)
    line[2] = column_sums(g3[0, pl.ds(PAD, all3), :] * diag3)
    ratio = None
    for x in range(columns):
        low, high = line[0, pl.ds(x, 1), :], line[2, pl.ds(x, 1), :]
        den = low + high
        if ratio is not None:
            den = den - low * ratio
        inv = 1.0 / den
        ratio = high * inv
        line[0, pl.ds(x, 1), :] = low * inv
        line[1, pl.ds(x, 1), :] = inv
        line[2, pl.ds(x, 1), :] = ratio

    for pair in halos:
        arrived(pair)
    first_sweep(s0, b0, w0, modes, PAD + rows, (width + 6) * rows, 16)
    sweep(a0, s0, s0, g0, modes, PAD + 2 * rows, (width + 4) * rows, 16, rows)
    sweep(d0, a0, s0, g0, modes, own0, size0, 16, rows, inverse=i0)

    pairs1 = b1.shape[0]
    for p in range(pairs1):
        left = pair_xy(d0.at[2 * p], own0, width, rows, temp)
        right = pair_xy(d0.at[2 * p + 1], own0, width, rows, temp)
        b1[p, pl.ds(own1, size1), :] = restrict_pair(left, right, merge)
    b1_halos = [
        to_neighbour(b1.at[:, pl.ds(own1, size1)], b1.at[:, pl.ds(own1 - size1, size1)], 1),
        to_neighbour(b1.at[:, pl.ds(own1, size1)], b1.at[:, pl.ds(own1 + size1, size1)], -1),
    ]
    for pair in b1_halos:
        arrived(pair)
    first_sweep(s1, b1, w1, pairs1, PAD + r1, (n1 + 8) * r1, 16)
    sweep(a1, s1, s1, g1, pairs1, PAD + 2 * r1, (n1 + 6) * r1, 16, r1)
    sweep(d1, a1, s1, g1, pairs1, own1, size1, 16, r1, inverse=i1)
    pairs2 = b2.shape[0]
    for p in range(pairs2):
        left = pair_xy(d1.at[2 * p], own1, n1, r1, temp)
        right = pair_xy(d1.at[2 * p + 1], own1, n1, r1, temp)
        b2[p, pl.ds(own2, size2), :] = restrict_pair(left, right, merge)
    row_copies = []
    for q in range(1, ROW):
        at = pl.ds(own2, size2)
        copy = start_copy(b2.at[:, at], b2.at[:, at], row_peer(q))
        sends.append((copy, None))
        row_copies.append((copy, None))
    for pair in row_copies:
        arrived(pair)
    col_copies = []
    for q in range(1, cols):
        at = pl.ds(group2, ROW * size2)
        copy = start_copy(b2.at[:, at], b2.at[:, at], col_peer(q))
        sends.append((copy, None))
        col_copies.append((copy, None))
    for pair in col_copies:
        arrived(pair)

    first_sweep(s2, b2, w2, pairs2, PAD, all2, 32)
    sweep(a2, s2, s2, g2, pairs2, PAD, all2, 32, r2)
    sweep(d2, a2, s2, g2, pairs2, PAD, all2, 32, r2, inverse=i2)
    left = pair_xy(d2.at[0], PAD, blocks * n2, r2, temp)
    right = pair_xy(d2.at[1], PAD, blocks * n2, r2, temp)
    b3[0, pl.ds(PAD, all3), :] = restrict_pair(left, right, merge)
    first_sweep(s3, b3, w3, 1, PAD, all3, 32)
    now, other = s3, a3
    for turn in range(COARSE - 1):
        sweep(other, now, s3, g3, 1, PAD, all3, 32, r3)
        now, other = (a3, d3) if now is s3 else (other, now)
    sweep(b3, now, s3, g3, 1, PAD, all3, 32, r3, inverse=i3)
    sums[...] = column_sums(b3[0, pl.ds(PAD, all3), :])
    carried = None
    for x in range(columns):
        value = sums[pl.ds(x, 1), :] * line[1, pl.ds(x, 1), :]
        if carried is not None:
            value = value + line[0, pl.ds(x, 1), :] * carried
        sums[pl.ds(x, 1), :] = value
        carried = value
    carried = None
    for x in reversed(range(columns)):
        value = sums[pl.ds(x, 1), :]
        if carried is not None:
            value = value + line[2, pl.ds(x, 1), :] * carried
        carried = value
        at = pl.ds(PAD + x * r3, r3)
        now[0, at, :] = now[0, at, :] + jnp.broadcast_to(value, (r3, LANES))
    prolong(a2, pairs2, PAD, now, PAD, columns, r3, spread, temp)
    sweep(d2, a2, s2, g2, pairs2, PAD, all2, 32, r2)
    sweep(a2, d2, s2, g2, pairs2, PAD, all2, 32, r2)
    window = pl.multiple_of(PAD + me * size2 - 2 * r2, 8)
    prolong(a1, pairs1, PAD + r1, a2, window, n2 + 4, r2, spread, temp)
    sweep(d1, a1, s1, g1, pairs1, PAD + 3 * r1, (n1 + 4) * r1, 16, r1)
    sweep(a1, d1, s1, g1, pairs1, PAD + 4 * r1, (n1 + 2) * r1, 16, r1)
    prolong(a0, modes, PAD + 2 * rows, a1, PAD + 4 * r1, n1 + 2, r1, spread, temp)
    sweep(d0, a0, s0, g0, modes, PAD + 3 * rows, (width + 2) * rows, 16, rows)
    sweep(a0, d0, s0, g0, modes, own0, size0, 16, rows)
    for m in range(modes):
        out_ref[m] = a0[m, pl.ds(own0, size0), :]
    for copy, exists in sends:
        if exists is None:
            copy.wait_send()
        else:
            pl.when(exists)(copy.wait_send)


def vcycle(residual, fields, blocks):
    modes, width, rows, depth = residual.shape
    plane = width * rows
    even = modes + modes % 2
    r1, r2, r3 = rows // 2, rows // 4, rows // 8
    grid = width * blocks
    n0 = (width + 8) * rows + 2 * PAD
    n1 = (width // 2 + 10) * r1 + 2 * PAD
    n2 = grid // 4 * r2 + 2 * PAD
    n3 = grid // 8 * r3 + 2 * PAD
    scratch = []
    for size, count in ((n0, even), (n1, even // 2), (n2, even // 4), (n3, 1)):
        scratch += [pltpu.VMEM((size, LANES), F32)] * 3
        scratch += [pltpu.VMEM((6, size, LANES), F32)]
        scratch += [pltpu.VMEM((count, size, LANES), F32)] * 4
    copies = 4 + 4 + 2 + 2 * (ROW - 1 + blocks // ROW - 1)
    scratch += [
        pltpu.VMEM((grid // 4 * r2, LANES), F32),
        pltpu.VMEM((3, grid // 8, LANES), F32),
        pltpu.VMEM((grid // 8, LANES), F32),
        pltpu.SemaphoreType.DMA((copies,)),
        pltpu.SemaphoreType.DMA((copies,)),
    ]
    geometry = (modes, width, rows, blocks)
    out = pl.pallas_call(
        lambda *refs: cycle_kernel(geometry, *refs),
        out_shape=jax.ShapeDtypeStruct((modes, plane, depth), F32),
        in_specs=[pl.BlockSpec(memory_space=pltpu.VMEM)] * 2,
        out_specs=pl.BlockSpec(memory_space=pltpu.VMEM),
        scratch_shapes=scratch,
        compiler_params=pltpu.CompilerParams(
            collective_id=1, has_side_effects=True, vmem_limit_bytes=56 * 2**20),
        name="vcycle",
    )(residual.reshape(modes, plane, depth), fields[0:1].reshape(1, plane, depth))
    return out.reshape(residual.shape)


def padded(cells, sides, width):
    for axis, dim in sides:
        count = lax.axis_size(axis)
        ends = count - 1
        head = lax.slice_in_dim(cells, 0, width, axis=dim)
        tail = lax.slice_in_dim(cells, cells.shape[dim] - width, cells.shape[dim], axis=dim)
        cells = jnp.concatenate(
            [
                lax.ppermute(tail, axis, [(i, (i + 1) % count) for i in range(ends)]),
                cells,
                lax.ppermute(head, axis, [((i + 1) % count, i) for i in range(ends)]),
            ],
            axis=dim,
        )
    return cells


def along_last(values, offset):
    size = values.shape[-1]
    zeros = jnp.zeros(values.shape[:-1] + (abs(offset),), values.dtype)
    if offset > 0:
        return jnp.concatenate([values[..., offset:], zeros], axis=-1)
    return jnp.concatenate([zeros, values[..., : size + offset]], axis=-1)


def neighbours(values_rim, depth):
    values = values_rim[..., 1:-1, :]
    positions = lax.iota(jnp.int32, values.shape[-1]) % depth
    upper = positions < depth - 1
    lower = positions > 0
    others = (
        values_rim[..., 2:, :],
        values_rim[..., :-2, :],
        along_last(values, depth),
        along_last(values, -depth),
        jnp.where(upper, along_last(values, 1), 0.0),
        jnp.where(lower, along_last(values, -1), 0.0),
    )
    return (values, others)


def faces_of(field_rim, depth):
    field, others = neighbours(field_rim, depth)
    plane = field.shape[-1]
    places = lax.iota(jnp.int32, plane)
    within = places % depth
    inside = (places < plane - depth, places >= depth, within < depth - 1, within > 0)
    collected = [0.5 * (field + others[0]), 0.5 * (field + others[1])]
    for keep, other in zip(inside, others[2:]):
        collected.append(jnp.where(keep, 0.5 * (field + other), 0.0))
    return collected


def apply_operator(faces, values_rim, scale, depth):
    values, others = neighbours(values_rim, depth)
    total = faces[0] * (values - others[0])
    for face, other in zip(faces[1:], others[1:]):
        total = total + face * (values - other)
    return scale * total


def diagonal_of(faces, scale):
    total = faces[0]
    for face in faces[1:]:
        total = total + face
    return scale * total


def coupling_tables(coupling_list):
    modes = jnp.arange(P_SIZE, dtype=jnp.int32)
    orders = jnp.arange(1, KL + 1, dtype=jnp.int32)
    firsts = (coupling_list[0][:, None] == modes[None, :]).astype(jnp.float32)
    seconds = (coupling_list[1][:, None] == modes[None, :]).astype(jnp.float32)
    weights = jnp.sqrt(coupling_list[3].astype(jnp.float32))
    which = (coupling_list[2][:, None] == orders[None, :]).astype(jnp.float32) * weights[:, None]
    return jnp.einsum("nk,ni,nj->kij", which, firsts, seconds, precision=lax.Precision.HIGHEST)


def local(blocks, pressure, source, kl_field, coupling_list):
    local_modes, width, rows, depth = pressure.shape
    plane = rows * depth
    pressure = pressure.reshape(local_modes, width, plane)
    source = source.reshape(local_modes, width, plane)
    fields = kl_field.reshape(kl_field.shape[0], width, plane)
    joined = padded(jnp.concatenate([pressure, fields], axis=0), (("space", 1),), 1)
    pressure_rim = joined[:local_modes]
    field_rim = joined[local_modes:]
    mean_faces = faces_of(field_rim[0:1], depth)
    spread_faces = faces_of(field_rim[1:, None], depth)
    image = apply_operator(mean_faces, pressure_rim, 1.0, depth)
    tables = coupling_tables(coupling_list)
    first = lax.axis_index("mode") * local_modes
    own_rows = lax.dynamic_slice_in_dim(tables, first, local_modes, axis=1)
    mixed = jnp.einsum(
        "kij,jxn->kixn",
        own_rows,
        lax.all_gather(pressure, "mode", axis=0, tiled=True),
        precision=lax.Precision.HIGHEST,
    )
    mixed_rim = padded(mixed.reshape(KL * local_modes, width, plane), (("space", 1),), 1)
    mixed_rim = mixed_rim.reshape(KL, local_modes, width + 2, plane)
    coupled = jnp.sum(apply_operator(spread_faces, mixed_rim, 1.0, depth), axis=0)
    residual = source - (image + coupled)
    shape = (local_modes, width, rows, depth)
    residual = residual.reshape(shape)
    return (vcycle(residual, kl_field, blocks), residual)


def solution(mesh):
    in_specs = (
        P("mode", "space", None, None),
        P("mode", "space", None, None),
        P(None, "space", None, None),
        P(),
    )
    out_specs = (P("mode", "space", None, None), P("mode", "space", None, None))
    blocks = mesh.shape["space"]
    return jax.shard_map(lambda *arrays: local(blocks, *arrays), mesh=mesh, in_specs=in_specs, out_specs=out_specs, check_vma=False)
```

```python
import jax
import jax.numpy as jnp
from jax import lax
from jax.sharding import PartitionSpec as P
from jax.experimental import pallas as pl
from jax.experimental.pallas import tpu as pltpu

MESH = pl.DeviceIdType.MESH
F32 = jnp.float32
P_SIZE = 56
KL = 5
RING = 4
CHUNKS = ((7, 1), (0, 1), (1, 2), (5, 2), (3, 2))
SWEEPS = 2
COARSE = 8
LEVELS = 4
LANES = 128
ROW = 8
COLS = 4
PAD = 16


def split_dot(values, matrix):
    high = values.astype(jnp.bfloat16)
    low = (values - high.astype(F32)).astype(jnp.bfloat16)
    return jnp.dot(high, matrix, preferred_element_type=F32) + jnp.dot(
        low, matrix, preferred_element_type=F32
    )


def pairing():
    wide = lax.broadcasted_iota(jnp.int32, (2 * LANES, LANES), 0)
    narrow = lax.broadcasted_iota(jnp.int32, (2 * LANES, LANES), 1)
    return jnp.where(wide // 2 == narrow, 1.0, 0.0).astype(jnp.bfloat16)


def spreading():
    narrow = lax.broadcasted_iota(jnp.int32, (LANES, 2 * LANES), 0)
    wide = lax.broadcasted_iota(jnp.int32, (LANES, 2 * LANES), 1)
    return jnp.where(wide // 2 == narrow, 1.0, 0.0).astype(jnp.bfloat16)


def level_faces(coef, faces, weight, inverse, first, count, step, rows, depth, scale, origin, width):
    bits = rows.bit_length() - 1
    lane = lax.broadcasted_iota(jnp.int32, (step, LANES), 1) & (depth - 1)
    place = lax.broadcasted_iota(jnp.int32, (step, LANES), 0)

    @pl.loop(0, count // step)
    def _(turn):
        base = pl.multiple_of(first + turn * step, 8)
        at = place + (base - PAD)
        y = at & (rows - 1)
        x = (at >> bits) + origin
        inside = jnp.logical_and(x >= 0, x < width)
        c = coef[pl.ds(base, step), :]
        others = (
            (coef[pl.ds(base + rows, step), :], None),
            (coef[pl.ds(base - rows, step), :], None),
            (coef[pl.ds(base + 1, step), :], y < rows - 1),
            (coef[pl.ds(base - 1, step), :], y > 0),
            (pltpu.roll(c, LANES - 1, 1), lane < depth - 1),
            (pltpu.roll(c, 1, 1), lane > 0),
        )
        sides = []
        total = jnp.zeros_like(c)
        for other, keep in others:
            face = 0.5 * (c + other)
            if keep is not None:
                face = jnp.where(keep, face, 0.0)
            sides.append(face)
            total = total + face
        part = jnp.where(inside, 0.8 / jnp.where(inside, total, 1.0), 0.0)
        weight[pl.ds(base, step), :] = part * (1.0 / scale)
        inverse[pl.ds(base, step), :] = jnp.where(inside, total * (scale * 1.25), 0.0)
        for n in range(6):
            faces[n, pl.ds(base, step), :] = part * sides[n]


def first_sweep(start, right, weight, modes, first, count, step):
    @pl.loop(0, count // step)
    def _(turn):
        base = pl.multiple_of(first + turn * step, 8)
        w = weight[pl.ds(base, step), :]
        for m in range(modes):
            start[m, pl.ds(base, step), :] = w * right[m, pl.ds(base, step), :]


def sweep(out, now, start, faces, modes, first, count, step, rows, keep=0.2, inverse=None):
    @pl.loop(0, count // step)
    def _(turn):
        base = pl.multiple_of(first + turn * step, 8)
        g = [faces[n, pl.ds(base, step), :] for n in range(6)]
        for m in range(modes):
            c = now[m, pl.ds(base, step), :]
            total = start[m, pl.ds(base, step), :] + (keep if inverse is None else -0.8) * c
            total = total + g[0] * now[m, pl.ds(base + rows, step), :]
            total = total + g[1] * now[m, pl.ds(base - rows, step), :]
            total = total + g[2] * now[m, pl.ds(base + 1, step), :]
            total = total + g[3] * now[m, pl.ds(base - 1, step), :]
            total = total + g[4] * pltpu.roll(c, LANES - 1, 1)
            total = total + g[5] * pltpu.roll(c, 1, 1)
            if inverse is not None:
                total = total * inverse[pl.ds(base, step), :]
            out[m, pl.ds(base, step), :] = total


def pair_xy(values, first, planes, rows, temp):
    for x in range(planes // 2):
        temp[pl.ds(x * rows, rows), :] = (
            values[pl.ds(first + 2 * x * rows, rows), :]
            + values[pl.ds(first + (2 * x + 1) * rows, rows), :]
        )
    half = planes // 2 * rows // 2
    return temp[pl.ds(0, half, 2), :] + temp[pl.ds(1, half, 2), :]


def restrict_pair(left, right, matrix):
    return 0.125 * split_dot(jnp.concatenate([left, right], axis=-1), matrix)


def prolong(fine, modes, fine_first, coarse, coarse_first, planes, rows, matrix, temp):
    count = planes * rows
    for p in range((modes + 1) // 2):
        both = split_dot(coarse[p, pl.ds(coarse_first, count), :], matrix)
        for part in range(2):
            m = 2 * p + part
            if m >= modes:
                continue
            child = both[:, part * LANES : (part + 1) * LANES]
            temp[pl.ds(0, count, 2), :] = child
            temp[pl.ds(1, count, 2), :] = child
            for x in range(planes):
                child_plane = temp[pl.ds(2 * x * rows, 2 * rows), :]
                for side in range(2):
                    at = pl.ds(fine_first + (2 * x + side) * 2 * rows, 2 * rows)
                    fine[m, at, :] = fine[m, at, :] + child_plane


def zero_all(ref):
    ref[...] = jnp.zeros(ref.shape, ref.dtype)


def cycle_kernel(
    geometry, place_ref, share_ref, p_ref, source_ref, field_ref, out_ref, residual_ref,
    c0, w0, i0, g0, b0, s0, a0, d0,
    c1, w1, i1, g1, b1, s1, a1, d1,
    c2, w2, i2, g2, b2, s2, a2, d2,
    c3, w3, i3, g3, b3, s3, a3, d3,
    temp, line, sums,
    q0, q1, q2, q3, q4, rim_low, rim_high, spread_fields, face_x, face_y, face_z,
    mix_a, mix_b, mix_c, mix_d, mix_e, mix_f, hold_a, hold_b, hold_c, partial, arriving,
    send_sem, recv_sem,
):
    modes, width, rows, blocks = geometry
    grid = width * blocks
    me = lax.axis_index("space")
    mode = lax.axis_index("mode")
    r1, r2, r3 = rows // 2, rows // 4, rows // 8
    n1, n2 = width // 2, width // 4
    row_at, col_at = me % ROW, me // ROW
    cols = blocks // ROW
    counter = [0]

    def start_copy(src, dst, target, exists=None, other_mode=None):
        number = counter[0]
        counter[0] += 1
        copy = pltpu.make_async_remote_copy(
            src_ref=src, dst_ref=dst, send_sem=send_sem.at[number], recv_sem=recv_sem.at[number],
            device_id=(target, mode if other_mode is None else other_mode), device_id_type=MESH,
        )
        if exists is None:
            copy.start()
        else:
            pl.when(exists)(copy.start)
        return copy

    def shift_exists(delta):
        return me + delta < blocks if delta > 0 else me + delta >= 0

    sends = []

    def to_neighbour(src, dst, delta):
        copy = start_copy(src, dst, me + delta, shift_exists(delta))
        sends.append((copy, shift_exists(delta)))
        return (copy, shift_exists(-delta))

    def arrived(pair):
        copy, exists = pair
        if exists is None:
            copy.wait_recv()
        else:
            pl.when(exists)(copy.wait_recv)

    def row_peer(q):
        return col_at * ROW + (row_at + q) % ROW

    def col_peer(q):
        return ((col_at + q) % cols) * ROW + row_at

    own0 = PAD + 4 * rows
    size0 = width * rows
    for ref in (c0, c1, b1):
        zero_all(ref)
    for at in (pl.ds(own0 - 3 * rows, 3 * rows), pl.ds(own0 + size0, 3 * rows)):
        b0[:, at, :] = jnp.zeros((b0.shape[0], 3 * rows, LANES), F32)
    spread_fields[...] = jnp.zeros(spread_fields.shape, F32)

    @pl.when(me == 0)
    def _():
        zero_all(rim_low)

    @pl.when(me == blocks - 1)
    def _():
        zero_all(rim_high)

    barrier = pltpu.get_barrier_semaphore()
    expected = ROW - 1 + cols - 1
    for delta in (1, -1, 2, -2):
        @pl.when(shift_exists(delta))
        def _():
            pl.semaphore_signal(barrier, inc=1, device_id=(me + delta, mode), device_id_type=MESH)
        expected = expected + jnp.where(shift_exists(delta), 1, 0)
    for q in range(1, ROW):
        pl.semaphore_signal(barrier, inc=1, device_id=(row_peer(q), mode), device_id_type=MESH)
    for q in range(1, cols):
        pl.semaphore_signal(barrier, inc=1, device_id=(col_peer(q), mode), device_id_type=MESH)
    y = mode // 2
    partner = y * 2 + 1 - mode % 2
    up, down = (mode + 2) % (2 * RING), (mode + 2 * RING - 2) % (2 * RING)
    for other in (up, down, partner):
        pl.semaphore_signal(barrier, inc=1, device_id=(me, other), device_id_type=MESH)
    expected = expected + 3
    own_slot = pl.ds(y * modes, modes)
    parts = (q0, q1, q2, q3, q4)
    for (plane, count), part in zip(CHUNKS, parts):
        for m in range(modes):
            part[y * modes + m] = p_ref[m, pl.ds(plane * rows, count * rows), :]
    pl.semaphore_wait(barrier, expected)

    def slot(distance, first=0, count=modes):
        return pl.ds((y + RING + distance) % RING * modes + first, count)

    near, far = {}, {}

    def send_own(c):
        plane, count = CHUNKS[c]
        src = p_ref.at[:, pl.ds(plane * rows, count * rows)]
        dst = parts[c].at[own_slot]
        near[c] = (start_copy(src, dst, me, None, up), start_copy(src, dst, me, None, down))
        sends.extend((copy, None) for copy in near[c])

    def pass_on(c):
        cut = modes // 2 + (c + 1) % 2
        near[c][0].wait_recv()
        at = parts[c].at[slot(-1, 0, cut)]
        first = start_copy(at, at, me, None, up)
        near[c][1].wait_recv()
        at = parts[c].at[slot(1, cut, modes - cut)]
        far[c] = (first, start_copy(at, at, me, None, down))
        sends.extend((copy, None) for copy in far[c])

    def complete(c):
        far[c][0].wait_recv()
        far[c][1].wait_recv()

    send_own(0)
    send_own(1)

    c_halos = []
    c_halos.append(to_neighbour(field_ref.at[0, pl.ds(size0 - 4 * rows, 4 * rows)], c0.at[pl.ds(own0 - 4 * rows, 4 * rows)], 1))
    c_halos.append(to_neighbour(field_ref.at[0, pl.ds(0, 4 * rows)], c0.at[pl.ds(own0 + size0, 4 * rows)], -1))
    own_f = PAD + rows
    c_halos.append(to_neighbour(field_ref.at[pl.ds(1, KL), pl.ds(size0 - rows, rows)], spread_fields.at[:, pl.ds(PAD, rows)], 1))
    c_halos.append(to_neighbour(field_ref.at[pl.ds(1, KL), pl.ds(0, rows)], spread_fields.at[:, pl.ds(own_f + size0, rows)], -1))
    c0[pl.ds(own0, size0), :] = field_ref[0]
    for k in range(KL):
        spread_fields[k, pl.ds(own_f, size0), :] = field_ref[k + 1]
    for mix in (mix_a, mix_b, mix_c, mix_d, mix_e, mix_f):
        mix[:, pl.ds(rows, 8), :] = jnp.zeros((mix.shape[0], 8, LANES), F32)
    for pair in c_halos:
        arrived(pair)

    @pl.loop(0, width + 1)
    def _(turn):
        lane = lax.broadcasted_iota(jnp.int32, (rows, LANES), 1)
        line_at = lax.broadcasted_iota(jnp.int32, (rows, LANES), 0)
        base = pl.multiple_of(turn * rows, 8)
        for k in range(KL + 1):
            ref = c0 if k == 0 else spread_fields.at[k - 1]
            shift = own0 - rows if k == 0 else PAD
            here = ref[pl.ds(shift + base, rows), :]
            face_x[k, pl.ds(base, rows), :] = 0.5 * (here + ref[pl.ds(shift + base + rows, rows), :])
            face_y[k, pl.ds(base, rows), :] = jnp.where(
                line_at < rows - 1, 0.5 * (here + ref[pl.ds(shift + base + 1, rows), :]), 0.0)
            face_z[k, pl.ds(base, rows), :] = jnp.where(
                lane < LANES - 1, 0.5 * (here + pltpu.roll(here, LANES - 1, 1)), 0.0)

    def source_of(x):
        if x < 0:
            return rim_low, 0
        if x >= width:
            return rim_high, 0
        for (plane, count), part in zip(CHUNKS, parts):
            if plane <= x < plane + count:
                return part, (x - plane) * rows

    def mixed(t, k, x):
        ref, at = source_of(x)
        entry = t * KL + k
        return (
            share_ref[0, entry] * ref[place_ref[0, entry], pl.ds(at, rows), :]
            + share_ref[1, entry] * ref[place_ref[1, entry], pl.ds(at, rows), :]
        )

    def fill(first, fields, now, x):
        @pl.loop(0, modes)
        def _(t):
            for k in range(KL):
                now[t * fields + k, pl.ds(0, rows), :] = mixed(first + t, k, x)
            if fields > KL:
                ref, at = source_of(x)
                now[t * fields + KL, pl.ds(0, rows), :] = ref[y * modes + t, pl.ds(at, rows), :]

    def advance(first, fields, now, later, hold, x, emit):
        here = pl.ds((x + 1) * rows, rows)

        @pl.loop(0, modes)
        def _(t):
            along_x = jnp.zeros((rows, LANES), F32)
            along_y, along_z = along_x, along_x
            for k in range(fields):
                if k < KL:
                    field = k + 1
                    value = mixed(first + t, k, x + 1)
                else:
                    field = 0
                    ref, at = source_of(x + 1)
                    value = ref[y * modes + t, pl.ds(at, rows), :]
                at = t * fields + k
                later[at, pl.ds(0, rows), :] = value
                old = now[at, pl.ds(0, rows), :]
                along_x = along_x + face_x[field, here, :] * (old - value)
                if emit is not None:
                    along_y = along_y + face_y[field, here, :] * (old - now[at, pl.ds(1, rows), :])
                    along_z = along_z + face_z[field, here, :] * (old - pltpu.roll(old, LANES - 1, 1))
            if emit is not None:
                emit(t, along_x - hold[t] + (along_y - pltpu.roll(along_y, 1, 0))
                     + (along_z - pltpu.roll(along_z, 1, 1)))
            hold[t] = along_x

    to_partner = {}

    def send_partner(x):
        to_partner[x] = start_copy(partial.at[x], arriving.at[x], me, None, partner)
        sends.append((to_partner[x], None))

    def emit_partner(x):
        def emit(t, value):
            partial[x, t] = value
        return emit

    def emit_own(x):
        def emit(t, value):
            at = pl.ds(own0 + x * rows, rows)
            b0[t, at, :] = source_ref[t, pl.ds(x * rows, rows), :] - value
        return emit

    def partner_step(now, later, hold, x, emits=True):
        advance(modes, KL, now, later, hold, x, emit_partner(x) if emits else None)

    last = width - 1
    pass_on(0)
    send_own(2)
    pass_on(1)
    send_own(3)
    complete(0)
    low = to_neighbour(q0, rim_low, 1)
    complete(1)
    high = to_neighbour(q1, rim_high, -1)
    pass_on(2)
    send_own(4)
    complete(2)
    arrived(low)
    fill(modes, KL, mix_a, -1)
    partner_step(mix_a, mix_b, hold_a, -1, False)
    partner_step(mix_b, mix_a, hold_a, 0)
    send_partner(0)
    pass_on(3)
    partner_step(mix_a, mix_b, hold_a, 1)
    send_partner(1)
    complete(3)
    arrived(high)
    fill(modes, KL, mix_c, 5)
    partner_step(mix_c, mix_d, hold_b, 5, False)
    partner_step(mix_d, mix_c, hold_b, 6)
    send_partner(6)
    pass_on(4)
    partner_step(mix_c, mix_d, hold_b, 7)
    send_partner(7)
    complete(4)
    partner_step(mix_b, mix_a, hold_a, 2)
    send_partner(2)
    partner_step(mix_a, mix_b, hold_a, 3)
    partner_step(mix_b, mix_a, hold_a, 4)
    partner_step(mix_a, mix_b, hold_a, 5)
    send_partner(5)
    send_partner(3)
    send_partner(4)
    fill(0, KL + 1, mix_e, -1)
    now, later = mix_e, mix_f
    for x in range(-1, width):
        advance(0, KL + 1, now, later, hold_c, x, emit_own(x) if x >= 0 else None)
        now, later = later, now
    for ref in (s0, a0, d0, s1, a1, d1, s2, a2, d2, s3, a3, d3):
        zero_all(ref)
    for ref in (c2, c3):
        ref[pl.ds(0, PAD), :] = jnp.zeros((PAD, LANES), F32)
        ref[pl.ds(ref.shape[0] - PAD, PAD), :] = jnp.zeros((PAD, LANES), F32)

    merge = pairing()
    spread = spreading()

    own1 = PAD + 5 * r1
    size1 = n1 * r1
    part = pair_xy(c0, own0, width, rows, temp)
    c1[pl.ds(own1, size1), :] = restrict_pair(part, part, merge)
    c1_halos = [
        to_neighbour(c1.at[pl.ds(own1, size1)], c1.at[pl.ds(own1 - size1, size1)], 1),
        to_neighbour(c1.at[pl.ds(own1, size1)], c1.at[pl.ds(own1 + size1, size1)], -1),
        to_neighbour(c1.at[pl.ds(own1 + size1 - r1, r1)], c1.at[pl.ds(own1 - size1 - r1, r1)], 2),
        to_neighbour(c1.at[pl.ds(own1, r1)], c1.at[pl.ds(own1 + 2 * size1, r1)], -2),
    ]
    size2 = n2 * r2
    own2 = pl.multiple_of(PAD + me * size2, 8)
    group2 = pl.multiple_of(PAD + col_at * (ROW * size2), 8)
    part = pair_xy(c1, own1, n1, r1, temp)
    c2[pl.ds(own2, size2), :] = restrict_pair(part, part, merge)
    c2_row = []
    for q in range(1, ROW):
        copy = start_copy(c2.at[pl.ds(own2, size2)], c2.at[pl.ds(own2, size2)], row_peer(q))
        sends.append((copy, None))
        c2_row.append((copy, None))

    level_faces(c0, g0, w0, i0, PAD + rows, (width + 6) * rows, 16, rows, LANES, 1.0, me * width - 4, grid)

    for pair in c2_row:
        arrived(pair)
    c2_col = []
    for q in range(1, cols):
        at = pl.ds(group2, ROW * size2)
        copy = start_copy(c2.at[at], c2.at[at], col_peer(q))
        sends.append((copy, None))
        c2_col.append((copy, None))
    for pair in c1_halos:
        arrived(pair)
    level_faces(c1, g1, w1, i1, PAD + r1, (n1 + 8) * r1, 16, r1, LANES // 2, 0.25, me * n1 - 5, grid // 2)
    for pair in c2_col:
        arrived(pair)
    all2 = blocks * size2
    level_faces(c2, g2, w2, i2, PAD, all2, 32, r2, LANES // 4, 0.0625, 0, grid // 4)
    part = pair_xy(c2, PAD, blocks * n2, r2, temp)
    all3 = all2 // 4
    c3[pl.ds(PAD, all3), :] = restrict_pair(part, part, merge)
    level_faces(c3, g3, w3, i3, PAD, all3, 32, r3, LANES // 8, 0.015625, 0, grid // 8)
    columns = grid // 8
    gather = jnp.where(
        lax.broadcasted_iota(jnp.int32, (columns, all3), 1) // r3
        == lax.broadcasted_iota(jnp.int32, (columns, all3), 0), 1.0, 0.0)
    within = jnp.where(
        lax.broadcasted_iota(jnp.int32, (LANES, LANES), 1) // (LANES // 8)
        == lax.broadcasted_iota(jnp.int32, (LANES, LANES), 0) // (LANES // 8), 1.0, 0.0)

    def column_sums(values):
        return jnp.dot(
            jnp.dot(gather, values, precision=lax.Precision.HIGHEST, preferred_element_type=F32),
            within, precision=lax.Precision.HIGHEST, preferred_element_type=F32)

    diag3 = i3[pl.ds(PAD, all3), :]
    line[0] = column_sums(g3[1, pl.ds(PAD, all3), :] * diag3)
    line[2] = column_sums(g3[0, pl.ds(PAD, all3), :] * diag3)
    ratio = None
    for x in range(columns):
        low, high = line[0, pl.ds(x, 1), :], line[2, pl.ds(x, 1), :]
        den = low + high
        if ratio is not None:
            den = den - low * ratio
        inv = 1.0 / den
        ratio = high * inv
        line[0, pl.ds(x, 1), :] = low * inv
        line[1, pl.ds(x, 1), :] = inv
        line[2, pl.ds(x, 1), :] = ratio

    def receive(x):
        to_partner[x].wait_recv()
        at = pl.ds(own0 + x * rows, rows)
        for m in range(modes):
            value = b0[m, at, :] - arriving[x, m]
            b0[m, at, :] = value
            residual_ref[m, pl.ds(x * rows, rows), :] = value

    halos = []
    for x in (0, 1, 2):
        receive(x)
    halos.append(to_neighbour(b0.at[pl.ds(0, modes), pl.ds(own0, 3 * rows)], b0.at[pl.ds(0, modes), pl.ds(own0 + size0, 3 * rows)], -1))
    for x in (6, 7, 5):
        receive(x)
    halos.append(to_neighbour(b0.at[pl.ds(0, modes), pl.ds(own0 + size0 - 3 * rows, 3 * rows)], b0.at[pl.ds(0, modes), pl.ds(own0 - 3 * rows, 3 * rows)], 1))
    for x in (3, 4):
        receive(x)
    for pair in halos:
        arrived(pair)
    first_sweep(s0, b0, w0, modes, PAD + rows, (width + 6) * rows, 16)
    sweep(a0, s0, s0, g0, modes, PAD + 2 * rows, (width + 4) * rows, 16, rows)
    sweep(d0, a0, s0, g0, modes, own0, size0, 16, rows, inverse=i0)

    pairs1 = b1.shape[0]
    for p in range(pairs1):
        left = pair_xy(d0.at[2 * p], own0, width, rows, temp)
        right = pair_xy(d0.at[2 * p + 1], own0, width, rows, temp)
        b1[p, pl.ds(own1, size1), :] = restrict_pair(left, right, merge)
    b1_halos = [
        to_neighbour(b1.at[:, pl.ds(own1, size1)], b1.at[:, pl.ds(own1 - size1, size1)], 1),
        to_neighbour(b1.at[:, pl.ds(own1, size1)], b1.at[:, pl.ds(own1 + size1, size1)], -1),
    ]
    for pair in b1_halos:
        arrived(pair)
    first_sweep(s1, b1, w1, pairs1, PAD + r1, (n1 + 8) * r1, 16)
    sweep(a1, s1, s1, g1, pairs1, PAD + 2 * r1, (n1 + 6) * r1, 16, r1)
    sweep(d1, a1, s1, g1, pairs1, own1, size1, 16, r1, inverse=i1)
    pairs2 = b2.shape[0]
    for p in range(pairs2):
        left = pair_xy(d1.at[2 * p], own1, n1, r1, temp)
        right = pair_xy(d1.at[2 * p + 1], own1, n1, r1, temp)
        b2[p, pl.ds(own2, size2), :] = restrict_pair(left, right, merge)
    row_copies = []
    for q in range(1, ROW):
        at = pl.ds(own2, size2)
        copy = start_copy(b2.at[:, at], b2.at[:, at], row_peer(q))
        sends.append((copy, None))
        row_copies.append((copy, None))
    for pair in row_copies:
        arrived(pair)
    col_copies = []
    for q in range(1, cols):
        at = pl.ds(group2, ROW * size2)
        copy = start_copy(b2.at[:, at], b2.at[:, at], col_peer(q))
        sends.append((copy, None))
        col_copies.append((copy, None))
    for pair in col_copies:
        arrived(pair)

    first_sweep(s2, b2, w2, pairs2, PAD, all2, 32)
    sweep(a2, s2, s2, g2, pairs2, PAD, all2, 32, r2)
    sweep(d2, a2, s2, g2, pairs2, PAD, all2, 32, r2, inverse=i2)
    left = pair_xy(d2.at[0], PAD, blocks * n2, r2, temp)
    right = pair_xy(d2.at[1], PAD, blocks * n2, r2, temp)
    b3[0, pl.ds(PAD, all3), :] = restrict_pair(left, right, merge)
    first_sweep(s3, b3, w3, 1, PAD, all3, 32)
    now, other = s3, a3
    for turn in range(COARSE - 1):
        sweep(other, now, s3, g3, 1, PAD, all3, 32, r3)
        now, other = (a3, d3) if now is s3 else (other, now)
    sweep(b3, now, s3, g3, 1, PAD, all3, 32, r3, inverse=i3)
    sums[...] = column_sums(b3[0, pl.ds(PAD, all3), :])
    carried = None
    for x in range(columns):
        value = sums[pl.ds(x, 1), :] * line[1, pl.ds(x, 1), :]
        if carried is not None:
            value = value + line[0, pl.ds(x, 1), :] * carried
        sums[pl.ds(x, 1), :] = value
        carried = value
    carried = None
    for x in reversed(range(columns)):
        value = sums[pl.ds(x, 1), :]
        if carried is not None:
            value = value + line[2, pl.ds(x, 1), :] * carried
        carried = value
        at = pl.ds(PAD + x * r3, r3)
        now[0, at, :] = now[0, at, :] + jnp.broadcast_to(value, (r3, LANES))
    prolong(a2, pairs2, PAD, now, PAD, columns, r3, spread, temp)
    sweep(d2, a2, s2, g2, pairs2, PAD, all2, 32, r2)
    sweep(a2, d2, s2, g2, pairs2, PAD, all2, 32, r2)
    window = pl.multiple_of(PAD + me * size2 - 2 * r2, 8)
    prolong(a1, pairs1, PAD + r1, a2, window, n2 + 4, r2, spread, temp)
    sweep(d1, a1, s1, g1, pairs1, PAD + 3 * r1, (n1 + 4) * r1, 16, r1)
    sweep(a1, d1, s1, g1, pairs1, PAD + 4 * r1, (n1 + 2) * r1, 16, r1)
    prolong(a0, modes, PAD + 2 * rows, a1, PAD + 4 * r1, n1 + 2, r1, spread, temp)
    sweep(d0, a0, s0, g0, modes, PAD + 3 * rows, (width + 2) * rows, 16, rows)
    sweep(a0, d0, s0, g0, modes, own0, size0, 16, rows)
    for m in range(modes):
        out_ref[m] = a0[m, pl.ds(own0, size0), :]
    for copy, exists in sends:
        if exists is None:
            copy.wait_send()
        else:
            pl.when(exists)(copy.wait_send)


def coupling_places(coupling_list, mode, modes):
    side = mode % 2
    targets = jnp.concatenate([
        mode * modes + jnp.arange(modes, dtype=jnp.int32),
        (mode + 1 - 2 * side) * modes + jnp.arange(modes, dtype=jnp.int32),
    ])
    wanted = (targets[:, None] * 8 + jnp.arange(1, KL + 1, dtype=jnp.int32)[None, :]).reshape(-1)
    given = coupling_list[0] * 8 + coupling_list[2]
    other = coupling_list[1]
    held = (other // modes) % 2 == side
    slot = other // (2 * modes) * modes + other % modes
    match = jnp.logical_and(wanted[:, None] == given[None, :], held[None, :])
    code = jnp.where(match, slot * 4 + coupling_list[3], -1)
    high = jnp.max(code, axis=1)
    low = jnp.min(jnp.where(match, slot * 4 + coupling_list[3], 1 << 20), axis=1)
    low = jnp.where(low < high, low, 0)
    both = jnp.maximum(jnp.stack([high, low]), 0)
    return both // 4, jnp.sqrt((both % 4).astype(F32))


def local(blocks, pressure, source, kl_field, coupling_list):
    modes, width, rows, depth = pressure.shape
    plane = width * rows
    even = modes + modes % 2
    r1, r2, r3 = rows // 2, rows // 4, rows // 8
    grid = width * blocks
    n0 = (width + 8) * rows + 2 * PAD
    n1 = (width // 2 + 10) * r1 + 2 * PAD
    n2 = grid // 4 * r2 + 2 * PAD
    n3 = grid // 8 * r3 + 2 * PAD
    scratch = []
    for size, count in ((n0, even), (n1, even // 2), (n2, even // 4), (n3, 1)):
        scratch += [pltpu.VMEM((size, LANES), F32)] * 3
        scratch += [pltpu.VMEM((6, size, LANES), F32)]
        scratch += [pltpu.VMEM((count, size, LANES), F32)] * 4
    cycle_copies = 4 + 4 + 2 + 2 * (ROW - 1 + blocks // ROW - 1)
    copies = cycle_copies + 4 * len(CHUNKS) + 4 + width
    held = RING * modes
    scratch += [
        pltpu.VMEM((grid // 4 * r2, LANES), F32),
        pltpu.VMEM((3, grid // 8, LANES), F32),
        pltpu.VMEM((grid // 8, LANES), F32),
    ]
    scratch += [pltpu.VMEM((held, count * rows, LANES), F32) for _, count in CHUNKS]
    scratch += [pltpu.VMEM((held, rows, LANES), F32)] * 2
    scratch += [pltpu.VMEM((KL, (width + 2) * rows + 2 * PAD, LANES), F32)]
    scratch += [pltpu.VMEM((KL + 1, (width + 1) * rows, LANES), F32)] * 3
    scratch += [pltpu.VMEM((modes * KL, rows + 8, LANES), F32)] * 4
    scratch += [pltpu.VMEM((modes * (KL + 1), rows + 8, LANES), F32)] * 2
    scratch += [pltpu.VMEM((modes, rows, LANES), F32)] * 3
    scratch += [pltpu.VMEM((width, modes, rows, LANES), F32)] * 2
    scratch += [pltpu.SemaphoreType.DMA((copies,))] * 2
    geometry = (modes, width, rows, blocks)
    places, shares = coupling_places(coupling_list, lax.axis_index("mode"), modes)
    shape = jax.ShapeDtypeStruct((modes, plane, depth), F32)
    out, residual = pl.pallas_call(
        lambda *refs: cycle_kernel(geometry, *refs),
        out_shape=(shape, shape),
        in_specs=[pl.BlockSpec(memory_space=pltpu.SMEM)] * 2 + [pl.BlockSpec(memory_space=pltpu.VMEM)] * 3,
        out_specs=[pl.BlockSpec(memory_space=pltpu.VMEM)] * 2,
        scratch_shapes=scratch,
        compiler_params=pltpu.CompilerParams(
            collective_id=1, has_side_effects=True, vmem_limit_bytes=60 * 2**20),
        name="coupled_cycle",
    )(places, shares, pressure.reshape(modes, plane, depth), source.reshape(modes, plane, depth),
      kl_field.reshape(KL + 1, plane, depth))
    return (out.reshape(pressure.shape), residual.reshape(pressure.shape))


def solution(mesh):
    in_specs = (
        P("mode", "space", None, None),
        P("mode", "space", None, None),
        P(None, "space", None, None),
        P(),
    )
    out_specs = (P("mode", "space", None, None), P("mode", "space", None, None))
    blocks = mesh.shape["space"]
    return jax.shard_map(lambda *arrays: local(blocks, *arrays), mesh=mesh, in_specs=in_specs, out_specs=out_specs, check_vma=False)
```

```python
import jax
import jax.numpy as jnp
from jax import lax
from jax.sharding import PartitionSpec as P
from jax.experimental import pallas as pl
from jax.experimental.pallas import tpu as pltpu

MESH = pl.DeviceIdType.MESH
F32 = jnp.float32
P_SIZE = 56
KL = 5
RING = 4
CHUNKS = ((7, 1), (0, 1), (1, 1), (2, 1), (6, 1), (5, 1), (3, 1), (4, 1))
COPIES = 96
NEAR = (1, -1, 2, -2, 3, -3)
SWEEPS = 2
COARSE = 8
LEVELS = 4
LANES = 128
ROW = 8
COLS = 4
PAD = 16


def split_dot(values, matrix):
    high = values.astype(jnp.bfloat16)
    low = (values - high.astype(F32)).astype(jnp.bfloat16)
    return jnp.dot(high, matrix, preferred_element_type=F32) + jnp.dot(
        low, matrix, preferred_element_type=F32
    )


def pairing():
    wide = lax.broadcasted_iota(jnp.int32, (2 * LANES, LANES), 0)
    narrow = lax.broadcasted_iota(jnp.int32, (2 * LANES, LANES), 1)
    return jnp.where(wide // 2 == narrow, 1.0, 0.0).astype(jnp.bfloat16)


def spreading():
    narrow = lax.broadcasted_iota(jnp.int32, (LANES, 2 * LANES), 0)
    wide = lax.broadcasted_iota(jnp.int32, (LANES, 2 * LANES), 1)
    return jnp.where(wide // 2 == narrow, 1.0, 0.0).astype(jnp.bfloat16)


def level_faces(coef, faces, weight, inverse, first, count, step, rows, depth, scale, origin, width):
    bits = rows.bit_length() - 1
    lane = lax.broadcasted_iota(jnp.int32, (step, LANES), 1) & (depth - 1)
    place = lax.broadcasted_iota(jnp.int32, (step, LANES), 0)

    @pl.loop(0, count // step)
    def _(turn):
        base = pl.multiple_of(first + turn * step, 8)
        at = place + (base - PAD)
        y = at & (rows - 1)
        x = (at >> bits) + origin
        inside = jnp.logical_and(x >= 0, x < width)
        c = coef[pl.ds(base, step), :]
        others = (
            (coef[pl.ds(base + rows, step), :], None),
            (coef[pl.ds(base - rows, step), :], None),
            (coef[pl.ds(base + 1, step), :], y < rows - 1),
            (coef[pl.ds(base - 1, step), :], y > 0),
            (pltpu.roll(c, LANES - 1, 1), lane < depth - 1),
            (pltpu.roll(c, 1, 1), lane > 0),
        )
        sides = []
        total = jnp.zeros_like(c)
        for other, keep in others:
            face = 0.5 * (c + other)
            if keep is not None:
                face = jnp.where(keep, face, 0.0)
            sides.append(face)
            total = total + face
        part = jnp.where(inside, 0.8 / jnp.where(inside, total, 1.0), 0.0)
        weight[pl.ds(base, step), :] = part * (1.0 / scale)
        inverse[pl.ds(base, step), :] = jnp.where(inside, total * (scale * 1.25), 0.0)
        for n in range(6):
            faces[n, pl.ds(base, step), :] = part * sides[n]


def first_sweep(start, right, weight, modes, first, count, step):
    @pl.loop(0, count // step)
    def _(turn):
        base = pl.multiple_of(first + turn * step, 8)
        w = weight[pl.ds(base, step), :]
        for m in range(modes):
            start[m, pl.ds(base, step), :] = w * right[m, pl.ds(base, step), :]


def sweep(out, now, start, faces, modes, first, count, step, rows, keep=0.2, inverse=None):
    @pl.loop(0, count // step)
    def _(turn):
        base = pl.multiple_of(first + turn * step, 8)
        g = [faces[n, pl.ds(base, step), :] for n in range(6)]
        for m in range(modes):
            c = now[m, pl.ds(base, step), :]
            total = start[m, pl.ds(base, step), :] + (keep if inverse is None else -0.8) * c
            total = total + g[0] * now[m, pl.ds(base + rows, step), :]
            total = total + g[1] * now[m, pl.ds(base - rows, step), :]
            total = total + g[2] * now[m, pl.ds(base + 1, step), :]
            total = total + g[3] * now[m, pl.ds(base - 1, step), :]
            total = total + g[4] * pltpu.roll(c, LANES - 1, 1)
            total = total + g[5] * pltpu.roll(c, 1, 1)
            if inverse is not None:
                total = total * inverse[pl.ds(base, step), :]
            out[m, pl.ds(base, step), :] = total


def pair_xy(values, first, planes, rows, temp):
    for x in range(planes // 2):
        temp[pl.ds(x * rows, rows), :] = (
            values[pl.ds(first + 2 * x * rows, rows), :]
            + values[pl.ds(first + (2 * x + 1) * rows, rows), :]
        )
    half = planes // 2 * rows // 2
    return temp[pl.ds(0, half, 2), :] + temp[pl.ds(1, half, 2), :]


def restrict_pair(left, right, matrix):
    return 0.125 * split_dot(jnp.concatenate([left, right], axis=-1), matrix)


def prolong(fine, modes, fine_first, coarse, planes, rows, matrix, temp):
    count = planes * rows
    for p in range((modes + 1) // 2):
        both = split_dot(coarse(p), matrix)
        for part in range(2):
            m = 2 * p + part
            if m >= modes:
                continue
            child = both[:, part * LANES : (part + 1) * LANES]
            temp[pl.ds(0, count, 2), :] = child
            temp[pl.ds(1, count, 2), :] = child
            for x in range(planes):
                child_plane = temp[pl.ds(2 * x * rows, 2 * rows), :]
                for side in range(2):
                    at = pl.ds(fine_first + (2 * x + side) * 2 * rows, 2 * rows)
                    fine[m, at, :] = fine[m, at, :] + child_plane


def zero_all(ref):
    ref[...] = jnp.zeros(ref.shape, ref.dtype)


def cycle_kernel(
    geometry, place_ref, share_ref, p_ref, source_ref, field_ref, out_ref, residual_ref,
    c0, w0, i0, g0, b0, s0, a0, d0,
    c1, w1, i1, g1, b1, s1, a1, d1,
    c2, w2, i2, g2, b2, s2, a2, d2,
    c3, w3, i3, g3, b3, s3, a3, d3,
    temp, line, sums,
    small, slots, q0, q1, q2, q3, q4, q5, q6, q7, rim_low, rim_high, spread_fields, face_x, face_y, face_z,
    mix_a, mix_b, mix_c, mix_d, mix_e, mix_f, hold_a, hold_b, hold_c, partial, arriving,
    send_sem, recv_sem,
):
    modes, width, rows, blocks = geometry
    grid = width * blocks
    me = lax.axis_index("space")
    mode = lax.axis_index("mode")
    r1, r2, r3 = rows // 2, rows // 4, rows // 8
    n1, n2 = width // 2, width // 4
    row_at, col_at = me % ROW, me // ROW
    cols = blocks // ROW
    counter = [0]

    def start_copy(src, dst, target, exists=None, other_mode=None):
        number = counter[0]
        counter[0] += 1
        copy = pltpu.make_async_remote_copy(
            src_ref=src, dst_ref=dst, send_sem=send_sem.at[number], recv_sem=recv_sem.at[number],
            device_id=(target, mode if other_mode is None else other_mode), device_id_type=MESH,
        )
        if exists is None:
            copy.start()
        else:
            pl.when(exists)(copy.start)
        return copy

    def finish():
        for m in range(modes):
            out_ref[m] = a0[m, pl.ds(own0, size0), :]
        for copy, exists in sends:
            if exists is None:
                copy.wait_send()
            else:
                pl.when(exists)(copy.wait_send)

    def shift_exists(delta):
        return me + delta < blocks if delta > 0 else me + delta >= 0

    sends = []

    def to_neighbour(src, dst, delta):
        copy = start_copy(src, dst, me + delta, shift_exists(delta))
        sends.append((copy, shift_exists(delta)))
        return (copy, shift_exists(-delta))

    def arrived(pair):
        copy, exists = pair
        if exists is None:
            copy.wait_recv()
        else:
            pl.when(exists)(copy.wait_recv)

    def row_peer(q):
        return col_at * ROW + (row_at + q) % ROW

    def col_peer(q):
        return ((col_at + q) % cols) * ROW + row_at

    own0 = PAD + 4 * rows
    size0 = width * rows
    for ref in (c0, c1, b1, c2, b2, c3):
        zero_all(ref)
    for at in (pl.ds(own0 - 3 * rows, 3 * rows), pl.ds(own0 + size0, 3 * rows)):
        b0[:, at, :] = jnp.zeros((b0.shape[0], 3 * rows, LANES), F32)
    spread_fields[...] = jnp.zeros(spread_fields.shape, F32)

    @pl.when(me == 0)
    def _():
        zero_all(rim_low)

    @pl.when(me == blocks - 1)
    def _():
        zero_all(rim_high)

    barrier = pltpu.get_barrier_semaphore()
    expected = ROW - 1 + cols - 1
    for delta in NEAR:
        @pl.when(shift_exists(delta))
        def _():
            pl.semaphore_signal(barrier, inc=1, device_id=(me + delta, mode), device_id_type=MESH)
        expected = expected + jnp.where(shift_exists(delta), 1, 0)
    for q in range(1, ROW):
        pl.semaphore_signal(barrier, inc=1, device_id=(row_peer(q), mode), device_id_type=MESH)
    for q in range(1, cols):
        pl.semaphore_signal(barrier, inc=1, device_id=(col_peer(q), mode), device_id_type=MESH)
    y = mode // 2
    partner = y * 2 + 1 - mode % 2
    up, down = (mode + 2) % (2 * RING), (mode + 2 * RING - 2) % (2 * RING)
    for other in (up, down, partner):
        pl.semaphore_signal(barrier, inc=1, device_id=(me, other), device_id_type=MESH)
    expected = expected + 3
    own_slot = pl.ds(y * modes, modes)
    parts = (q0, q1, q2, q3, q4, q5, q6, q7)
    for (plane, count), part in zip(CHUNKS, parts):
        for m in range(modes):
            part[y * modes + m] = p_ref[m, pl.ds(plane * rows, count * rows), :]
    pl.semaphore_wait(barrier, expected)

    def slot(distance, first=0, count=modes):
        return pl.ds((y + RING + distance) % RING * modes + first, count)

    near, far = {}, {}

    def send_own(c):
        plane, count = CHUNKS[c]
        src = p_ref.at[:, pl.ds(plane * rows, count * rows)]
        dst = parts[c].at[own_slot]
        near[c] = (start_copy(src, dst, me, None, up), start_copy(src, dst, me, None, down))
        sends.extend((copy, None) for copy in near[c])

    def pass_on(c):
        cut = modes // 2 + (c + 1) % 2
        near[c][0].wait_recv()
        at = parts[c].at[slot(-1, 0, cut)]
        first = start_copy(at, at, me, None, up)
        near[c][1].wait_recv()
        at = parts[c].at[slot(1, cut, modes - cut)]
        far[c] = (first, start_copy(at, at, me, None, down))
        sends.extend((copy, None) for copy in far[c])

    def complete(c):
        far[c][0].wait_recv()
        far[c][1].wait_recv()

    send_own(0)
    send_own(1)

    c_halos = []
    c_halos.append(to_neighbour(field_ref.at[0, pl.ds(size0 - 4 * rows, 4 * rows)], c0.at[pl.ds(own0 - 4 * rows, 4 * rows)], 1))
    c_halos.append(to_neighbour(field_ref.at[0, pl.ds(0, 4 * rows)], c0.at[pl.ds(own0 + size0, 4 * rows)], -1))
    own_f = PAD + rows
    c_halos.append(to_neighbour(field_ref.at[pl.ds(1, KL), pl.ds(size0 - rows, rows)], spread_fields.at[:, pl.ds(PAD, rows)], 1))
    c_halos.append(to_neighbour(field_ref.at[pl.ds(1, KL), pl.ds(0, rows)], spread_fields.at[:, pl.ds(own_f + size0, rows)], -1))
    c0[pl.ds(own0, size0), :] = field_ref[0]
    for k in range(KL):
        spread_fields[k, pl.ds(own_f, size0), :] = field_ref[k + 1]
    for mix in (mix_a, mix_b, mix_c, mix_d, mix_e, mix_f):
        mix[:, pl.ds(rows, 8), :] = jnp.zeros((mix.shape[0], 8, LANES), F32)
    def all_faces():
        for pair in c_halos:
            arrived(pair)

        @pl.loop(0, width + 1)
        def _(turn):
            lane = lax.broadcasted_iota(jnp.int32, (rows, LANES), 1)
            line_at = lax.broadcasted_iota(jnp.int32, (rows, LANES), 0)
            base = pl.multiple_of(turn * rows, 8)
            for k in range(KL + 1):
                ref = c0 if k == 0 else spread_fields.at[k - 1]
                shift = own0 - rows if k == 0 else PAD
                here = ref[pl.ds(shift + base, rows), :]
                face_x[k, pl.ds(base, rows), :] = 0.5 * (here + ref[pl.ds(shift + base + rows, rows), :])
                face_y[k, pl.ds(base, rows), :] = jnp.where(
                    line_at < rows - 1, 0.5 * (here + ref[pl.ds(shift + base + 1, rows), :]), 0.0)
                face_z[k, pl.ds(base, rows), :] = jnp.where(
                    lane < LANES - 1, 0.5 * (here + pltpu.roll(here, LANES - 1, 1)), 0.0)

    def source_of(x):
        if x < 0:
            return rim_low, 0
        if x >= width:
            return rim_high, 0
        for (plane, count), part in zip(CHUNKS, parts):
            if plane <= x < plane + count:
                return part, (x - plane) * rows

    def mixed(t, k, x):
        ref, at = source_of(x)
        entry = t * KL + k
        return (
            share_ref[0, entry] * ref[place_ref[0, entry], pl.ds(at, rows), :]
            + share_ref[1, entry] * ref[place_ref[1, entry], pl.ds(at, rows), :]
        )

    def fill(first, fields, now, x):
        @pl.loop(0, modes)
        def _(t):
            for k in range(KL):
                now[t * fields + k, pl.ds(0, rows), :] = mixed(first + t, k, x)
            if fields > KL:
                ref, at = source_of(x)
                now[t * fields + KL, pl.ds(0, rows), :] = ref[y * modes + t, pl.ds(at, rows), :]

    def advance(first, fields, now, later, hold, x, emit):
        here = pl.ds((x + 1) * rows, rows)

        @pl.loop(0, modes)
        def _(t):
            along_x = jnp.zeros((rows, LANES), F32)
            along_y, along_z = along_x, along_x
            for k in range(fields):
                if k < KL:
                    field = k + 1
                    value = mixed(first + t, k, x + 1)
                else:
                    field = 0
                    ref, at = source_of(x + 1)
                    value = ref[y * modes + t, pl.ds(at, rows), :]
                at = t * fields + k
                later[at, pl.ds(0, rows), :] = value
                old = now[at, pl.ds(0, rows), :]
                along_x = along_x + face_x[field, here, :] * (old - value)
                if emit is not None:
                    along_y = along_y + face_y[field, here, :] * (old - now[at, pl.ds(1, rows), :])
                    along_z = along_z + face_z[field, here, :] * (old - pltpu.roll(old, LANES - 1, 1))
            if emit is not None:
                emit(t, along_x - hold[t] + (along_y - pltpu.roll(along_y, 1, 0))
                     + (along_z - pltpu.roll(along_z, 1, 1)))
            hold[t] = along_x

    to_partner = {}

    def send_partner(x):
        to_partner[x] = start_copy(partial.at[x], arriving.at[x], me, None, partner)
        sends.append((to_partner[x], None))

    def emit_partner(x):
        def emit(t, value):
            partial[x, t] = value
        return emit

    def emit_own(x):
        def emit(t, value):
            at = pl.ds(own0 + x * rows, rows)
            b0[t, at, :] = source_ref[t, pl.ds(x * rows, rows), :] - value
        return emit

    def partner_step(now, later, hold, x, emits=True):
        advance(modes, KL, now, later, hold, x, emit_partner(x) if emits else None)

    merge = pairing()
    spread = spreading()
    own1 = PAD + 5 * r1
    size1 = n1 * r1
    own2 = PAD + 6 * r2
    size2 = n2 * r2
    columns = grid // 8
    all3 = columns * r3

    def gather_small(value, dest, turn):
        slots[turn, row_at, pl.ds(0, r3), :] = value
        copies = []
        for q in range(1, ROW):
            copy = start_copy(slots.at[turn, row_at], slots.at[turn, row_at], row_peer(q))
            sends.append((copy, None))
            copies.append((copy, None))

        def second():
            for pair in copies:
                arrived(pair)
            first = pl.multiple_of(PAD + col_at * (ROW * r3), 8)
            for n in range(0, ROW, 2):
                dest[pl.ds(first + n * r3, 2 * r3), :] = jnp.concatenate(
                    [slots[turn, n, pl.ds(0, r3), :], slots[turn, n + 1, pl.ds(0, r3), :]], axis=0)
            at = pl.ds(first, ROW * r3)
            more = []
            for q in range(1, cols):
                copy = start_copy(dest.at[at], dest.at[at], col_peer(q))
                sends.append((copy, None))
                more.append((copy, None))
            return more

        return second

    def coarse_coefficients():
        part = pair_xy(c0, own0, width, rows, temp)
        c1[pl.ds(own1, size1), :] = restrict_pair(part, part, merge)
        found = [
            to_neighbour(c1.at[pl.ds(own1, size1)], c1.at[pl.ds(own1 - size1, size1)], 1),
            to_neighbour(c1.at[pl.ds(own1, size1)], c1.at[pl.ds(own1 + size1, size1)], -1),
            to_neighbour(c1.at[pl.ds(own1 + size1 - r1, r1)], c1.at[pl.ds(own1 - size1 - r1, r1)], 2),
            to_neighbour(c1.at[pl.ds(own1, r1)], c1.at[pl.ds(own1 + 2 * size1, r1)], -2),
        ]
        part = pair_xy(c1, own1, n1, r1, temp)
        c2[pl.ds(own2, size2), :] = restrict_pair(part, part, merge)
        for delta in NEAR:
            found.append(to_neighbour(c2.at[pl.ds(own2, size2)], c2.at[pl.ds(own2 - delta * size2, size2)], delta))
        part = pair_xy(c2, own2, n2, r2, temp)
        return found, gather_small(restrict_pair(part, part, merge), c3, 0)

    def column_sums(values):
        gather = jnp.where(
            lax.broadcasted_iota(jnp.int32, (columns, all3), 1) // r3
            == lax.broadcasted_iota(jnp.int32, (columns, all3), 0), 1.0, 0.0)
        within = jnp.where(
            lax.broadcasted_iota(jnp.int32, (LANES, LANES), 1) // (LANES // 8)
            == lax.broadcasted_iota(jnp.int32, (LANES, LANES), 0) // (LANES // 8), 1.0, 0.0)
        return jnp.dot(
            jnp.dot(gather, values, precision=lax.Precision.HIGHEST, preferred_element_type=F32),
            within, precision=lax.Precision.HIGHEST, preferred_element_type=F32)

    def line_factors():
        diag3 = i3[pl.ds(PAD, all3), :]
        line[0] = column_sums(g3[1, pl.ds(PAD, all3), :] * diag3)
        line[2] = column_sums(g3[0, pl.ds(PAD, all3), :] * diag3)
        ratio = None
        for x in range(columns):
            low, high = line[0, pl.ds(x, 1), :], line[2, pl.ds(x, 1), :]
            den = low + high
            if ratio is not None:
                den = den - low * ratio
            inv = 1.0 / den
            ratio = high * inv
            line[0, pl.ds(x, 1), :] = low * inv
            line[1, pl.ds(x, 1), :] = inv
            line[2, pl.ds(x, 1), :] = ratio

    all_faces()
    pass_on(0)
    send_own(2)
    coarse_halos, coarse_second = coarse_coefficients()
    pass_on(1)
    send_own(3)
    complete(0)
    low = to_neighbour(q0, rim_low, 1)
    for ref in (s3, a3, d3):
        zero_all(ref)
    pass_on(2)
    send_own(4)
    complete(1)
    high = to_neighbour(q1, rim_high, -1)
    for ref in (s2, a2, d2, s1, a1, d1):
        zero_all(ref)
    pass_on(3)
    send_own(5)
    complete(2)
    arrived(low)
    fill(modes, KL, mix_a, -1)
    partner_step(mix_a, mix_b, hold_a, -1, False)
    partner_step(mix_b, mix_a, hold_a, 0)
    send_partner(0)
    pass_on(4)
    send_own(6)
    c3_more = coarse_second()
    complete(3)
    partner_step(mix_a, mix_b, hold_a, 1)
    send_partner(1)
    pass_on(5)
    send_own(7)
    for pair in coarse_halos:
        arrived(pair)
    level_faces(c1, g1, w1, i1, PAD + r1, (n1 + 8) * r1, 16, r1, LANES // 2, 0.25, me * n1 - 5, grid // 2)
    level_faces(c2, g2, w2, i2, PAD + r2, (n2 + 10) * r2, 16, r2, LANES // 4, 0.0625, me * n2 - 6, grid // 4)
    pass_on(6)
    complete(4)
    complete(5)
    arrived(high)
    fill(modes, KL, mix_c, 5)
    partner_step(mix_c, mix_d, hold_b, 5, False)
    partner_step(mix_d, mix_c, hold_b, 6)
    send_partner(6)
    pass_on(7)
    partner_step(mix_c, mix_d, hold_b, 7)
    send_partner(7)
    complete(6)
    partner_step(mix_b, mix_a, hold_a, 2)
    send_partner(2)
    complete(7)
    partner_step(mix_a, mix_b, hold_a, 3)
    partner_step(mix_b, mix_a, hold_a, 4)
    partner_step(mix_a, mix_b, hold_a, 5)
    send_partner(5)
    fill(0, KL + 1, mix_e, -1)
    now, later = mix_e, mix_f
    for x in range(-1, width):
        advance(0, KL + 1, now, later, hold_c, x, emit_own(x) if x >= 0 else None)
        now, later = later, now
        if x == 1:
            send_partner(3)
            send_partner(4)
    level_faces(c0, g0, w0, i0, PAD + rows, (width + 6) * rows, 16, rows, LANES, 1.0, me * width - 4, grid)
    for pair in c3_more:
        arrived(pair)
    level_faces(c3, g3, w3, i3, PAD, all3, 32, r3, LANES // 8, 0.015625, 0, grid // 8)
    line_factors()
    for ref in (s0, a0, d0):
        zero_all(ref)

    def receive(x):
        to_partner[x].wait_recv()
        at = pl.ds(own0 + x * rows, rows)
        for m in range(modes):
            value = b0[m, at, :] - arriving[x, m]
            b0[m, at, :] = value
            residual_ref[m, pl.ds(x * rows, rows), :] = value

    halos = []
    for x in (0, 1, 2):
        receive(x)
    halos.append(to_neighbour(b0.at[pl.ds(0, modes), pl.ds(own0, 3 * rows)], b0.at[pl.ds(0, modes), pl.ds(own0 + size0, 3 * rows)], -1))
    for x in (6, 7, 5):
        receive(x)
    halos.append(to_neighbour(b0.at[pl.ds(0, modes), pl.ds(own0 + size0 - 3 * rows, 3 * rows)], b0.at[pl.ds(0, modes), pl.ds(own0 - 3 * rows, 3 * rows)], 1))
    for x in (3, 4):
        receive(x)
    first_sweep(s0, b0, w0, modes, own0, size0, 16)
    sweep(a0, s0, s0, g0, modes, own0 + rows, size0 - 2 * rows, 16, rows)
    for pair in halos:
        arrived(pair)
    for at in (own0 - 3 * rows, own0 + size0):
        first_sweep(s0, b0, w0, modes, at, 3 * rows, 16)
    for at in (own0 - 2 * rows, own0 + size0 - rows):
        sweep(a0, s0, s0, g0, modes, at, 3 * rows, 16, rows)
    sweep(d0, a0, s0, g0, modes, own0, size0, 16, rows, inverse=i0)
    pairs1 = b1.shape[0]
    for p in range(pairs1):
        left = pair_xy(d0.at[2 * p], own0, width, rows, temp)
        right = pair_xy(d0.at[2 * p + 1], own0, width, rows, temp)
        b1[p, pl.ds(own1, size1), :] = restrict_pair(left, right, merge)
    b1_halos = [
        to_neighbour(b1.at[:, pl.ds(own1, size1)], b1.at[:, pl.ds(own1 - size1, size1)], 1),
        to_neighbour(b1.at[:, pl.ds(own1, size1)], b1.at[:, pl.ds(own1 + size1, size1)], -1),
    ]
    for pair in b1_halos:
        arrived(pair)
    first_sweep(s1, b1, w1, pairs1, PAD + r1, (n1 + 8) * r1, 16)
    sweep(a1, s1, s1, g1, pairs1, PAD + 2 * r1, (n1 + 6) * r1, 16, r1)
    sweep(d1, a1, s1, g1, pairs1, own1, size1, 16, r1, inverse=i1)
    pairs2 = b2.shape[0]
    for p in range(pairs2):
        left = pair_xy(d1.at[2 * p], own1, n1, r1, temp)
        right = pair_xy(d1.at[2 * p + 1], own1, n1, r1, temp)
        b2[p, pl.ds(own2, size2), :] = restrict_pair(left, right, merge)
    b2_halos = []
    for delta in NEAR:
        b2_halos.append(to_neighbour(b2.at[:, pl.ds(own2, size2)], b2.at[:, pl.ds(own2 - delta * size2, size2)], delta))
    for pair in b2_halos:
        arrived(pair)
    first_sweep(s2, b2, w2, pairs2, PAD + r2, (n2 + 10) * r2, 16)
    sweep(a2, s2, s2, g2, pairs2, PAD + 2 * r2, (n2 + 8) * r2, 16, r2)
    sweep(d2, a2, s2, g2, pairs2, own2, size2, 16, r2, inverse=i2)
    left = pair_xy(d2.at[0], own2, n2, r2, temp)
    right = pair_xy(d2.at[1], own2, n2, r2, temp)
    second = gather_small(restrict_pair(left, right, merge), b3.at[0], 1)
    for pair in second():
        arrived(pair)
    first_sweep(s3, b3, w3, 1, PAD, all3, 32)
    now, other = s3, a3
    for turn in range(COARSE - 1):
        sweep(other, now, s3, g3, 1, PAD, all3, 32, r3)
        now, other = (a3, d3) if now is s3 else (other, now)
    sweep(other, now, s3, g3, 1, PAD, all3, 32, r3, inverse=i3)
    sums[...] = column_sums(other[0, pl.ds(PAD, all3), :])
    carried = None
    for x in range(columns):
        value = sums[pl.ds(x, 1), :] * line[1, pl.ds(x, 1), :]
        if carried is not None:
            value = value + line[0, pl.ds(x, 1), :] * carried
        sums[pl.ds(x, 1), :] = value
        carried = value
    carried = None
    for x in reversed(range(columns)):
        value = sums[pl.ds(x, 1), :]
        if carried is not None:
            value = value + line[2, pl.ds(x, 1), :] * carried
        carried = value
        at = pl.ds(PAD + x * r3, r3)
        now[0, at, :] = now[0, at, :] + jnp.broadcast_to(value, (r3, LANES))
    for x in range(5):
        small[pl.ds(x * r3, r3), :] = now[0, pl.ds(PAD + (me + x - 2) * r3, r3), :]
    prolong(a2, pairs2, PAD + 2 * r2, lambda p: small[pl.ds(0, 5 * r3), :], 5, r3, spread, temp)
    sweep(d2, a2, s2, g2, pairs2, PAD + 3 * r2, (n2 + 6) * r2, 16, r2)
    sweep(a2, d2, s2, g2, pairs2, PAD + 4 * r2, (n2 + 4) * r2, 16, r2)
    prolong(a1, pairs1, PAD + r1, lambda p: a2[p, pl.ds(PAD + 4 * r2, (n2 + 4) * r2), :], n2 + 4, r2, spread, temp)
    sweep(d1, a1, s1, g1, pairs1, PAD + 3 * r1, (n1 + 4) * r1, 16, r1)
    sweep(a1, d1, s1, g1, pairs1, PAD + 4 * r1, (n1 + 2) * r1, 16, r1)
    prolong(a0, modes, PAD + 2 * rows, lambda p: a1[p, pl.ds(PAD + 4 * r1, (n1 + 2) * r1), :], n1 + 2, r1, spread, temp)
    sweep(d0, a0, s0, g0, modes, PAD + 3 * rows, (width + 2) * rows, 16, rows)
    sweep(a0, d0, s0, g0, modes, own0, size0, 16, rows)
    finish()


def coupling_places(coupling_list, mode, modes):
    side = mode % 2
    targets = jnp.concatenate([
        mode * modes + jnp.arange(modes, dtype=jnp.int32),
        (mode + 1 - 2 * side) * modes + jnp.arange(modes, dtype=jnp.int32),
    ])
    wanted = (targets[:, None] * 8 + jnp.arange(1, KL + 1, dtype=jnp.int32)[None, :]).reshape(-1)
    given = coupling_list[0] * 8 + coupling_list[2]
    other = coupling_list[1]
    held = (other // modes) % 2 == side
    slot = other // (2 * modes) * modes + other % modes
    match = jnp.logical_and(wanted[:, None] == given[None, :], held[None, :])
    code = jnp.where(match, slot * 4 + coupling_list[3], -1)
    high = jnp.max(code, axis=1)
    low = jnp.min(jnp.where(match, slot * 4 + coupling_list[3], 1 << 20), axis=1)
    low = jnp.where(low < high, low, 0)
    both = jnp.maximum(jnp.stack([high, low]), 0)
    return both // 4, jnp.sqrt((both % 4).astype(F32))


def local(blocks, pressure, source, kl_field, coupling_list):
    modes, width, rows, depth = pressure.shape
    plane = width * rows
    even = modes + modes % 2
    r1, r2, r3 = rows // 2, rows // 4, rows // 8
    grid = width * blocks
    n0 = (width + 8) * rows + 2 * PAD
    n1 = (width // 2 + 10) * r1 + 2 * PAD
    n2 = (width // 4 + 12) * r2 + 2 * PAD
    n3 = grid // 8 * r3 + 2 * PAD
    scratch = []
    for size, count in ((n0, even), (n1, even // 2), (n2, even // 4), (n3, 1)):
        scratch += [pltpu.VMEM((size, LANES), F32)] * 3
        scratch += [pltpu.VMEM((6, size, LANES), F32)]
        scratch += [pltpu.VMEM((count, size, LANES), F32)] * 4
    held = RING * modes
    scratch += [
        pltpu.VMEM((512, LANES), F32),
        pltpu.VMEM((3, grid // 8, LANES), F32),
        pltpu.VMEM((grid // 8, LANES), F32),
        pltpu.VMEM((24, LANES), F32),
        pltpu.VMEM((2, ROW, 8, LANES), F32),
    ]
    scratch += [pltpu.VMEM((held, count * rows, LANES), F32) for _, count in CHUNKS]
    scratch += [pltpu.VMEM((held, rows, LANES), F32)] * 2
    scratch += [pltpu.VMEM((KL, (width + 2) * rows + 2 * PAD, LANES), F32)]
    scratch += [pltpu.VMEM((KL + 1, (width + 1) * rows, LANES), F32)] * 3
    scratch += [pltpu.VMEM((modes * KL, rows + 8, LANES), F32)] * 4
    scratch += [pltpu.VMEM((modes * (KL + 1), rows + 8, LANES), F32)] * 2
    scratch += [pltpu.VMEM((modes, rows, LANES), F32)] * 3
    scratch += [pltpu.VMEM((width, modes, rows, LANES), F32)] * 2
    scratch += [pltpu.SemaphoreType.DMA((COPIES,))] * 2
    geometry = (modes, width, rows, blocks)
    places, shares = coupling_places(coupling_list, lax.axis_index("mode"), modes)
    shape = jax.ShapeDtypeStruct((modes, plane, depth), F32)
    out, residual = pl.pallas_call(
        lambda *refs: cycle_kernel(geometry, *refs),
        out_shape=(shape, shape),
        in_specs=[pl.BlockSpec(memory_space=pltpu.SMEM)] * 2 + [pl.BlockSpec(memory_space=pltpu.VMEM)] * 3,
        out_specs=[pl.BlockSpec(memory_space=pltpu.VMEM)] * 2,
        scratch_shapes=scratch,
        compiler_params=pltpu.CompilerParams(
            collective_id=1, has_side_effects=True, vmem_limit_bytes=60 * 2**20),
        name="coupled_cycle",
    )(places, shares, pressure.reshape(modes, plane, depth), source.reshape(modes, plane, depth),
      kl_field.reshape(KL + 1, plane, depth))
    return (out.reshape(pressure.shape), residual.reshape(pressure.shape))


def solution(mesh):
    in_specs = (
        P("mode", "space", None, None),
        P("mode", "space", None, None),
        P(None, "space", None, None),
        P(),
    )
    out_specs = (P("mode", "space", None, None), P("mode", "space", None, None))
    blocks = mesh.shape["space"]
    return jax.shard_map(lambda *arrays: local(blocks, *arrays), mesh=mesh, in_specs=in_specs, out_specs=out_specs, check_vma=False)
```

```python
import jax
import jax.numpy as jnp
from jax import lax
from jax.sharding import PartitionSpec as P
from jax.experimental import pallas as pl
from jax.experimental.pallas import tpu as pltpu

MESH = pl.DeviceIdType.MESH
F32 = jnp.float32
P_SIZE = 56
KL = 5
RING = 4
CHUNKS = ((7, 1), (0, 1), (1, 1), (2, 1), (6, 1), (5, 1), (3, 1), (4, 1))
COPIES = 96
NEAR = (1, -1, 2, -2, 3, -3)
SWEEPS = 2
COARSE = 8
LEVELS = 4
LANES = 128
ROW = 8
COLS = 4
PAD = 16


def split_dot(values, matrix):
    high = values.astype(jnp.bfloat16)
    low = (values - high.astype(F32)).astype(jnp.bfloat16)
    return jnp.dot(high, matrix, preferred_element_type=F32) + jnp.dot(
        low, matrix, preferred_element_type=F32
    )


def pairing():
    wide = lax.broadcasted_iota(jnp.int32, (2 * LANES, LANES), 0)
    narrow = lax.broadcasted_iota(jnp.int32, (2 * LANES, LANES), 1)
    return jnp.where(wide // 2 == narrow, 1.0, 0.0).astype(jnp.bfloat16)


def spreading():
    narrow = lax.broadcasted_iota(jnp.int32, (LANES, 2 * LANES), 0)
    wide = lax.broadcasted_iota(jnp.int32, (LANES, 2 * LANES), 1)
    return jnp.where(wide // 2 == narrow, 1.0, 0.0).astype(jnp.bfloat16)


def level_faces(coef, faces, weight, inverse, first, count, step, rows, depth, scale, origin, width):
    bits = rows.bit_length() - 1
    lane = lax.broadcasted_iota(jnp.int32, (step, LANES), 1) & (depth - 1)
    place = lax.broadcasted_iota(jnp.int32, (step, LANES), 0)

    @pl.loop(0, count // step)
    def _(turn):
        base = pl.multiple_of(first + turn * step, 8)
        at = place + (base - PAD)
        y = at & (rows - 1)
        x = (at >> bits) + origin
        inside = jnp.logical_and(x >= 0, x < width)
        c = coef[pl.ds(base, step), :]
        others = (
            (coef[pl.ds(base + rows, step), :], None),
            (coef[pl.ds(base - rows, step), :], None),
            (coef[pl.ds(base + 1, step), :], y < rows - 1),
            (coef[pl.ds(base - 1, step), :], y > 0),
            (pltpu.roll(c, LANES - 1, 1), lane < depth - 1),
            (pltpu.roll(c, 1, 1), lane > 0),
        )
        sides = []
        total = jnp.zeros_like(c)
        for other, keep in others:
            face = 0.5 * (c + other)
            if keep is not None:
                face = jnp.where(keep, face, 0.0)
            sides.append(face)
            total = total + face
        part = jnp.where(inside, 0.8 / jnp.where(inside, total, 1.0), 0.0)
        weight[pl.ds(base, step), :] = part * (1.0 / scale)
        inverse[pl.ds(base, step), :] = jnp.where(inside, total * (scale * 1.25), 0.0)
        for n in range(6):
            faces[n, pl.ds(base, step), :] = part * sides[n]


def first_sweep(start, right, weight, modes, first, count, step):
    @pl.loop(0, count // step)
    def _(turn):
        base = pl.multiple_of(first + turn * step, 8)
        w = weight[pl.ds(base, step), :]
        for m in range(modes):
            start[m, pl.ds(base, step), :] = w * right[m, pl.ds(base, step), :]


def sweep(out, now, start, faces, modes, first, count, step, rows, keep=0.2, inverse=None):
    @pl.loop(0, count // step)
    def _(turn):
        base = pl.multiple_of(first + turn * step, 8)
        g = [faces[n, pl.ds(base, step), :] for n in range(6)]
        for m in range(modes):
            c = now[m, pl.ds(base, step), :]
            total = start[m, pl.ds(base, step), :] + (keep if inverse is None else -0.8) * c
            total = total + g[0] * now[m, pl.ds(base + rows, step), :]
            total = total + g[1] * now[m, pl.ds(base - rows, step), :]
            total = total + g[2] * now[m, pl.ds(base + 1, step), :]
            total = total + g[3] * now[m, pl.ds(base - 1, step), :]
            total = total + g[4] * pltpu.roll(c, LANES - 1, 1)
            total = total + g[5] * pltpu.roll(c, 1, 1)
            if inverse is not None:
                total = total * inverse[pl.ds(base, step), :]
            out[m, pl.ds(base, step), :] = total


def pair_xy(values, first, planes, rows, temp):
    for x in range(planes // 2):
        temp[pl.ds(x * rows, rows), :] = (
            values[pl.ds(first + 2 * x * rows, rows), :]
            + values[pl.ds(first + (2 * x + 1) * rows, rows), :]
        )
    half = planes // 2 * rows // 2
    return temp[pl.ds(0, half, 2), :] + temp[pl.ds(1, half, 2), :]


def restrict_pair(left, right, matrix):
    return 0.125 * split_dot(jnp.concatenate([left, right], axis=-1), matrix)


def prolong(fine, modes, fine_first, coarse, planes, rows, matrix, temp):
    count = planes * rows
    for p in range((modes + 1) // 2):
        both = split_dot(coarse(p), matrix)
        for part in range(2):
            m = 2 * p + part
            if m >= modes:
                continue
            child = both[:, part * LANES : (part + 1) * LANES]
            temp[pl.ds(0, count, 2), :] = child
            temp[pl.ds(1, count, 2), :] = child
            for x in range(planes):
                child_plane = temp[pl.ds(2 * x * rows, 2 * rows), :]
                for side in range(2):
                    at = pl.ds(fine_first + (2 * x + side) * 2 * rows, 2 * rows)
                    fine[m, at, :] = fine[m, at, :] + child_plane


def zero_all(ref):
    ref[...] = jnp.zeros(ref.shape, ref.dtype)


def cycle_kernel(
    geometry, place_ref, share_ref, p_ref, source_ref, field_ref, out_ref, residual_ref,
    c0, w0, i0, g0, b0, s0, a0, d0,
    c1, w1, i1, g1, b1, s1, a1, d1,
    c2, w2, i2, g2, b2, s2, a2, d2,
    c3, w3, i3, g3, b3, s3, a3, d3,
    temp, line, sums,
    small, slots, q0, q1, q2, q3, q4, q5, q6, q7, rim_low, rim_high, spread_fields, face_x, face_y, face_z,
    mix_a, mix_b, mix_c, mix_d, mix_e, mix_f, hold_a, hold_b, hold_c, partial, arriving,
    send_sem, recv_sem,
):
    modes, width, rows, blocks = geometry
    grid = width * blocks
    me = lax.axis_index("space")
    mode = lax.axis_index("mode")
    r1, r2, r3 = rows // 2, rows // 4, rows // 8
    n1, n2 = width // 2, width // 4
    row_at, col_at = me % ROW, me // ROW
    cols = blocks // ROW
    counter = [0]

    def start_copy(src, dst, target, exists=None, other_mode=None):
        number = counter[0]
        counter[0] += 1
        copy = pltpu.make_async_remote_copy(
            src_ref=src, dst_ref=dst, send_sem=send_sem.at[number], recv_sem=recv_sem.at[number],
            device_id=(target, mode if other_mode is None else other_mode), device_id_type=MESH,
        )
        if exists is None:
            copy.start()
        else:
            pl.when(exists)(copy.start)
        return copy

    def finish():
        for m in range(modes):
            out_ref[m] = a0[m, pl.ds(own0, size0), :]
        for copy, exists in sends:
            if exists is None:
                copy.wait_send()
            else:
                pl.when(exists)(copy.wait_send)

    def shift_exists(delta):
        return me + delta < blocks if delta > 0 else me + delta >= 0

    sends = []

    def to_neighbour(src, dst, delta):
        copy = start_copy(src, dst, me + delta, shift_exists(delta))
        sends.append((copy, shift_exists(delta)))
        return (copy, shift_exists(-delta))

    def arrived(pair):
        copy, exists = pair
        if exists is None:
            copy.wait_recv()
        else:
            pl.when(exists)(copy.wait_recv)

    def row_peer(q):
        return col_at * ROW + (row_at + q) % ROW

    def col_peer(q):
        return ((col_at + q) % cols) * ROW + row_at

    own0 = PAD + 4 * rows
    size0 = width * rows
    for ref in (c0, c1, b1, c2, b2, c3):
        zero_all(ref)
    for at in (pl.ds(own0 - 3 * rows, 3 * rows), pl.ds(own0 + size0, 3 * rows)):
        b0[:, at, :] = jnp.zeros((b0.shape[0], 3 * rows, LANES), F32)
    spread_fields[...] = jnp.zeros(spread_fields.shape, F32)

    @pl.when(me == 0)
    def _():
        zero_all(rim_low)

    @pl.when(me == blocks - 1)
    def _():
        zero_all(rim_high)

    barrier = pltpu.get_barrier_semaphore()
    expected = ROW - 1 + cols - 1
    for delta in NEAR:
        @pl.when(shift_exists(delta))
        def _():
            pl.semaphore_signal(barrier, inc=1, device_id=(me + delta, mode), device_id_type=MESH)
        expected = expected + jnp.where(shift_exists(delta), 1, 0)
    for q in range(1, ROW):
        pl.semaphore_signal(barrier, inc=1, device_id=(row_peer(q), mode), device_id_type=MESH)
    for q in range(1, cols):
        pl.semaphore_signal(barrier, inc=1, device_id=(col_peer(q), mode), device_id_type=MESH)
    y = mode // 2
    partner = y * 2 + 1 - mode % 2
    up, down = (mode + 2) % (2 * RING), (mode + 2 * RING - 2) % (2 * RING)
    for other in (up, down, partner):
        pl.semaphore_signal(barrier, inc=1, device_id=(me, other), device_id_type=MESH)
    expected = expected + 3
    own_slot = pl.ds(y * modes, modes)
    parts = (q0, q1, q2, q3, q4, q5, q6, q7)
    for (plane, count), part in zip(CHUNKS, parts):
        for m in range(modes):
            part[y * modes + m] = p_ref[m, pl.ds(plane * rows, count * rows), :]
    pl.semaphore_wait(barrier, expected)

    def slot(distance, first=0, count=modes):
        return pl.ds((y + RING + distance) % RING * modes + first, count)

    near, far = {}, {}

    def send_own(c):
        plane, count = CHUNKS[c]
        src = p_ref.at[:, pl.ds(plane * rows, count * rows)]
        dst = parts[c].at[own_slot]
        near[c] = (start_copy(src, dst, me, None, up), start_copy(src, dst, me, None, down))
        sends.extend((copy, None) for copy in near[c])

    def pass_on(c):
        cut = modes // 2 + (c + 1) % 2
        near[c][0].wait_recv()
        at = parts[c].at[slot(-1, 0, cut)]
        first = start_copy(at, at, me, None, up)
        near[c][1].wait_recv()
        at = parts[c].at[slot(1, cut, modes - cut)]
        far[c] = (first, start_copy(at, at, me, None, down))
        sends.extend((copy, None) for copy in far[c])

    def complete(c):
        far[c][0].wait_recv()
        far[c][1].wait_recv()

    send_own(0)
    send_own(1)

    c_halos = []
    c_halos.append(to_neighbour(field_ref.at[0, pl.ds(size0 - 4 * rows, 4 * rows)], c0.at[pl.ds(own0 - 4 * rows, 4 * rows)], 1))
    c_halos.append(to_neighbour(field_ref.at[0, pl.ds(0, 4 * rows)], c0.at[pl.ds(own0 + size0, 4 * rows)], -1))
    own_f = PAD + rows
    c_halos.append(to_neighbour(field_ref.at[pl.ds(1, KL), pl.ds(size0 - rows, rows)], spread_fields.at[:, pl.ds(PAD, rows)], 1))
    c_halos.append(to_neighbour(field_ref.at[pl.ds(1, KL), pl.ds(0, rows)], spread_fields.at[:, pl.ds(own_f + size0, rows)], -1))
    c0[pl.ds(own0, size0), :] = field_ref[0]
    for k in range(KL):
        spread_fields[k, pl.ds(own_f, size0), :] = field_ref[k + 1]
    for mix in (mix_a, mix_b, mix_c, mix_d, mix_e, mix_f):
        mix[:, pl.ds(rows, 8), :] = jnp.zeros((mix.shape[0], 8, LANES), F32)
    def all_faces():
        for pair in c_halos:
            arrived(pair)

        @pl.loop(0, width + 1)
        def _(turn):
            lane = lax.broadcasted_iota(jnp.int32, (rows, LANES), 1)
            line_at = lax.broadcasted_iota(jnp.int32, (rows, LANES), 0)
            base = pl.multiple_of(turn * rows, 8)
            for k in range(KL + 1):
                ref = c0 if k == 0 else spread_fields.at[k - 1]
                shift = own0 - rows if k == 0 else PAD
                here = ref[pl.ds(shift + base, rows), :]
                face_x[k, pl.ds(base, rows), :] = 0.5 * (here + ref[pl.ds(shift + base + rows, rows), :])
                face_y[k, pl.ds(base, rows), :] = jnp.where(
                    line_at < rows - 1, 0.5 * (here + ref[pl.ds(shift + base + 1, rows), :]), 0.0)
                face_z[k, pl.ds(base, rows), :] = jnp.where(
                    lane < LANES - 1, 0.5 * (here + pltpu.roll(here, LANES - 1, 1)), 0.0)

    def source_of(x):
        if x < 0:
            return rim_low, 0
        if x >= width:
            return rim_high, 0
        for (plane, count), part in zip(CHUNKS, parts):
            if plane <= x < plane + count:
                return part, (x - plane) * rows

    def mixed(t, k, x):
        ref, at = source_of(x)
        entry = t * KL + k
        return (
            share_ref[0, entry] * ref[place_ref[0, entry], pl.ds(at, rows), :]
            + share_ref[1, entry] * ref[place_ref[1, entry], pl.ds(at, rows), :]
        )

    def fill(first, fields, now, x):
        @pl.loop(0, modes)
        def _(t):
            for k in range(KL):
                now[t * fields + k, pl.ds(0, rows), :] = mixed(first + t, k, x)
            if fields > KL:
                ref, at = source_of(x)
                now[t * fields + KL, pl.ds(0, rows), :] = ref[y * modes + t, pl.ds(at, rows), :]

    def advance(first, fields, now, later, hold, x, emit):
        here = pl.ds((x + 1) * rows, rows)

        @pl.loop(0, modes)
        def _(t):
            along_x = jnp.zeros((rows, LANES), F32)
            along_y, along_z = along_x, along_x
            for k in range(fields):
                if k < KL:
                    field = k + 1
                    value = mixed(first + t, k, x + 1)
                else:
                    field = 0
                    ref, at = source_of(x + 1)
                    value = ref[y * modes + t, pl.ds(at, rows), :]
                at = t * fields + k
                later[at, pl.ds(0, rows), :] = value
                old = now[at, pl.ds(0, rows), :]
                along_x = along_x + face_x[field, here, :] * (old - value)
                if emit is not None:
                    along_y = along_y + face_y[field, here, :] * (old - now[at, pl.ds(1, rows), :])
                    along_z = along_z + face_z[field, here, :] * (old - pltpu.roll(old, LANES - 1, 1))
            if emit is not None:
                emit(t, along_x - hold[t] + (along_y - pltpu.roll(along_y, 1, 0))
                     + (along_z - pltpu.roll(along_z, 1, 1)))
            hold[t] = along_x

    to_partner = {}

    def send_partner(x):
        to_partner[x] = start_copy(partial.at[x], arriving.at[x], me, None, partner)
        sends.append((to_partner[x], None))

    def emit_partner(x):
        def emit(t, value):
            partial[x, t] = value
        return emit

    def emit_own(x):
        def emit(t, value):
            at = pl.ds(own0 + x * rows, rows)
            b0[t, at, :] = source_ref[t, pl.ds(x * rows, rows), :] - value
        return emit

    def partner_step(now, later, hold, x, emits=True):
        advance(modes, KL, now, later, hold, x, emit_partner(x) if emits else None)

    merge = pairing()
    spread = spreading()
    own1 = PAD + 5 * r1
    size1 = n1 * r1
    own2 = PAD + 6 * r2
    size2 = n2 * r2
    columns = grid // 8
    all3 = columns * r3

    def gather_small(value, dest, turn):
        slots[turn, row_at, pl.ds(0, r3), :] = value
        copies = []
        for q in range(1, ROW):
            copy = start_copy(slots.at[turn, row_at], slots.at[turn, row_at], row_peer(q))
            sends.append((copy, None))
            copies.append((copy, None))

        def second():
            for pair in copies:
                arrived(pair)
            first = pl.multiple_of(PAD + col_at * (ROW * r3), 8)
            for n in range(0, ROW, 2):
                dest[pl.ds(first + n * r3, 2 * r3), :] = jnp.concatenate(
                    [slots[turn, n, pl.ds(0, r3), :], slots[turn, n + 1, pl.ds(0, r3), :]], axis=0)
            at = pl.ds(first, ROW * r3)
            more = []
            for q in range(1, cols):
                copy = start_copy(dest.at[at], dest.at[at], col_peer(q))
                sends.append((copy, None))
                more.append((copy, None))
            return more

        return second

    def coarse_coefficients():
        part = pair_xy(c0, own0, width, rows, temp)
        c1[pl.ds(own1, size1), :] = restrict_pair(part, part, merge)
        found = [
            to_neighbour(c1.at[pl.ds(own1, size1)], c1.at[pl.ds(own1 - size1, size1)], 1),
            to_neighbour(c1.at[pl.ds(own1, size1)], c1.at[pl.ds(own1 + size1, size1)], -1),
            to_neighbour(c1.at[pl.ds(own1 + size1 - r1, r1)], c1.at[pl.ds(own1 - size1 - r1, r1)], 2),
            to_neighbour(c1.at[pl.ds(own1, r1)], c1.at[pl.ds(own1 + 2 * size1, r1)], -2),
        ]
        part = pair_xy(c1, own1, n1, r1, temp)
        c2[pl.ds(own2, size2), :] = restrict_pair(part, part, merge)
        for delta in NEAR:
            found.append(to_neighbour(c2.at[pl.ds(own2, size2)], c2.at[pl.ds(own2 - delta * size2, size2)], delta))
        part = pair_xy(c2, own2, n2, r2, temp)
        return found, gather_small(restrict_pair(part, part, merge), c3, 0)

    def column_sums(values):
        gather = jnp.where(
            lax.broadcasted_iota(jnp.int32, (columns, all3), 1) // r3
            == lax.broadcasted_iota(jnp.int32, (columns, all3), 0), 1.0, 0.0)
        within = jnp.where(
            lax.broadcasted_iota(jnp.int32, (LANES, LANES), 1) // (LANES // 8)
            == lax.broadcasted_iota(jnp.int32, (LANES, LANES), 0) // (LANES // 8), 1.0, 0.0)
        return jnp.dot(
            jnp.dot(gather, values, precision=lax.Precision.HIGHEST, preferred_element_type=F32),
            within, precision=lax.Precision.HIGHEST, preferred_element_type=F32)

    def line_factors():
        diag3 = i3[pl.ds(PAD, all3), :]
        line[0] = column_sums(g3[1, pl.ds(PAD, all3), :] * diag3)
        line[2] = column_sums(g3[0, pl.ds(PAD, all3), :] * diag3)
        ratio = None
        for x in range(columns):
            low, high = line[0, pl.ds(x, 1), :], line[2, pl.ds(x, 1), :]
            den = low + high
            if ratio is not None:
                den = den - low * ratio
            inv = 1.0 / den
            ratio = high * inv
            line[0, pl.ds(x, 1), :] = low * inv
            line[1, pl.ds(x, 1), :] = inv
            line[2, pl.ds(x, 1), :] = ratio

    all_faces()
    pass_on(0)
    send_own(2)
    coarse_halos, coarse_second = coarse_coefficients()
    pass_on(1)
    send_own(3)
    complete(0)
    low = to_neighbour(q0, rim_low, 1)
    for ref in (s3, a3, d3):
        zero_all(ref)
    pass_on(2)
    send_own(4)
    complete(1)
    high = to_neighbour(q1, rim_high, -1)
    for ref in (s2, a2, d2, s1, a1, d1):
        zero_all(ref)
    pass_on(3)
    send_own(5)
    complete(2)
    arrived(low)
    fill(modes, KL, mix_a, -1)
    partner_step(mix_a, mix_b, hold_a, -1, False)
    partner_step(mix_b, mix_a, hold_a, 0)
    send_partner(0)
    pass_on(4)
    send_own(6)
    c3_more = coarse_second()
    complete(3)
    partner_step(mix_a, mix_b, hold_a, 1)
    send_partner(1)
    pass_on(5)
    send_own(7)
    for pair in coarse_halos:
        arrived(pair)
    level_faces(c1, g1, w1, i1, PAD + r1, (n1 + 8) * r1, 16, r1, LANES // 2, 0.25, me * n1 - 5, grid // 2)
    level_faces(c2, g2, w2, i2, PAD + r2, (n2 + 10) * r2, 16, r2, LANES // 4, 0.0625, me * n2 - 6, grid // 4)
    pass_on(6)
    complete(4)
    complete(5)
    arrived(high)
    fill(modes, KL, mix_c, 5)
    partner_step(mix_c, mix_d, hold_b, 5, False)
    partner_step(mix_d, mix_c, hold_b, 6)
    send_partner(6)
    pass_on(7)
    partner_step(mix_c, mix_d, hold_b, 7)
    send_partner(7)
    complete(6)
    partner_step(mix_b, mix_a, hold_a, 2)
    send_partner(2)
    complete(7)
    partner_step(mix_a, mix_b, hold_a, 3)
    partner_step(mix_b, mix_a, hold_a, 4)
    partner_step(mix_a, mix_b, hold_a, 5)
    send_partner(5)
    fill(0, KL + 1, mix_e, -1)
    now, later = mix_e, mix_f
    for x in range(-1, width):
        advance(0, KL + 1, now, later, hold_c, x, emit_own(x) if x >= 0 else None)
        now, later = later, now
        if x == 1:
            send_partner(3)
            send_partner(4)
    level_faces(c0, g0, w0, i0, PAD + rows, (width + 6) * rows, 16, rows, LANES, 1.0, me * width - 4, grid)
    for pair in c3_more:
        arrived(pair)
    level_faces(c3, g3, w3, i3, PAD, all3, 32, r3, LANES // 8, 0.015625, 0, grid // 8)
    line_factors()
    for ref in (s0, a0, d0):
        zero_all(ref)

    def receive(x):
        to_partner[x].wait_recv()
        at = pl.ds(own0 + x * rows, rows)
        for m in range(modes):
            value = b0[m, at, :] - arriving[x, m]
            b0[m, at, :] = value
            residual_ref[m, pl.ds(x * rows, rows), :] = value

    halos = []
    for x in (0, 1, 2):
        receive(x)
    halos.append(to_neighbour(b0.at[pl.ds(0, modes), pl.ds(own0, 3 * rows)], b0.at[pl.ds(0, modes), pl.ds(own0 + size0, 3 * rows)], -1))
    for x in (6, 7, 5):
        receive(x)
    halos.append(to_neighbour(b0.at[pl.ds(0, modes), pl.ds(own0 + size0 - 3 * rows, 3 * rows)], b0.at[pl.ds(0, modes), pl.ds(own0 - 3 * rows, 3 * rows)], 1))
    for x in (3, 4):
        receive(x)
    first_sweep(s0, b0, w0, modes, own0, size0, 16)
    sweep(a0, s0, s0, g0, modes, own0 + rows, size0 - 2 * rows, 16, rows)
    for pair in halos:
        arrived(pair)
    for at in (own0 - 3 * rows, own0 + size0):
        first_sweep(s0, b0, w0, modes, at, 3 * rows, 16)
    for at in (own0 - 2 * rows, own0 + size0 - rows):
        sweep(a0, s0, s0, g0, modes, at, 3 * rows, 16, rows)
    sweep(d0, a0, s0, g0, modes, own0, size0, 16, rows, inverse=i0)
    pairs1 = b1.shape[0]
    for p in range(pairs1):
        left = pair_xy(d0.at[2 * p], own0, width, rows, temp)
        right = pair_xy(d0.at[2 * p + 1], own0, width, rows, temp)
        b1[p, pl.ds(own1, size1), :] = restrict_pair(left, right, merge)
    b1_halos = [
        to_neighbour(b1.at[:, pl.ds(own1, size1)], b1.at[:, pl.ds(own1 - size1, size1)], 1),
        to_neighbour(b1.at[:, pl.ds(own1, size1)], b1.at[:, pl.ds(own1 + size1, size1)], -1),
    ]
    for pair in b1_halos:
        arrived(pair)
    first_sweep(s1, b1, w1, pairs1, PAD + r1, (n1 + 8) * r1, 32)
    sweep(a1, s1, s1, g1, pairs1, PAD + 2 * r1, (n1 + 6) * r1, 32, r1)
    sweep(d1, a1, s1, g1, pairs1, own1, size1, 32, r1, inverse=i1)
    pairs2 = b2.shape[0]
    for p in range(pairs2):
        left = pair_xy(d1.at[2 * p], own1, n1, r1, temp)
        right = pair_xy(d1.at[2 * p + 1], own1, n1, r1, temp)
        b2[p, pl.ds(own2, size2), :] = restrict_pair(left, right, merge)
    b2_halos = []
    for delta in NEAR:
        b2_halos.append(to_neighbour(b2.at[:, pl.ds(own2, size2)], b2.at[:, pl.ds(own2 - delta * size2, size2)], delta))
    for pair in b2_halos:
        arrived(pair)
    first_sweep(s2, b2, w2, pairs2, PAD + r2, (n2 + 10) * r2, 48)
    sweep(a2, s2, s2, g2, pairs2, PAD + 2 * r2, (n2 + 8) * r2, 40, r2)
    sweep(d2, a2, s2, g2, pairs2, own2, size2, 16, r2, inverse=i2)
    left = pair_xy(d2.at[0], own2, n2, r2, temp)
    right = pair_xy(d2.at[1], own2, n2, r2, temp)
    second = gather_small(restrict_pair(left, right, merge), b3.at[0], 1)
    for pair in second():
        arrived(pair)
    first_sweep(s3, b3, w3, 1, PAD, all3, all3)
    now, other = s3, a3
    for turn in range(COARSE - 1):
        sweep(other, now, s3, g3, 1, PAD, all3, all3, r3)
        now, other = (a3, d3) if now is s3 else (other, now)
    sweep(other, now, s3, g3, 1, PAD, all3, all3, r3, inverse=i3)
    sums[...] = column_sums(other[0, pl.ds(PAD, all3), :])
    carried = None
    for x in range(columns):
        value = sums[pl.ds(x, 1), :] * line[1, pl.ds(x, 1), :]
        if carried is not None:
            value = value + line[0, pl.ds(x, 1), :] * carried
        sums[pl.ds(x, 1), :] = value
        carried = value
    carried = None
    for x in reversed(range(columns)):
        value = sums[pl.ds(x, 1), :]
        if carried is not None:
            value = value + line[2, pl.ds(x, 1), :] * carried
        carried = value
        at = pl.ds(PAD + x * r3, r3)
        now[0, at, :] = now[0, at, :] + jnp.broadcast_to(value, (r3, LANES))
    for x in range(5):
        small[pl.ds(x * r3, r3), :] = now[0, pl.ds(PAD + (me + x - 2) * r3, r3), :]
    prolong(a2, pairs2, PAD + 2 * r2, lambda p: small[pl.ds(0, 5 * r3), :], 5, r3, spread, temp)
    sweep(d2, a2, s2, g2, pairs2, PAD + 3 * r2, (n2 + 6) * r2, 32, r2)
    sweep(a2, d2, s2, g2, pairs2, PAD + 4 * r2, (n2 + 4) * r2, 48, r2)
    prolong(a1, pairs1, PAD + r1, lambda p: a2[p, pl.ds(PAD + 4 * r2, (n2 + 4) * r2), :], n2 + 4, r2, spread, temp)
    sweep(d1, a1, s1, g1, pairs1, PAD + 3 * r1, (n1 + 4) * r1, 32, r1)
    sweep(a1, d1, s1, g1, pairs1, PAD + 4 * r1, (n1 + 2) * r1, 32, r1)
    prolong(a0, modes, PAD + 2 * rows, lambda p: a1[p, pl.ds(PAD + 4 * r1, (n1 + 2) * r1), :], n1 + 2, r1, spread, temp)
    sweep(d0, a0, s0, g0, modes, PAD + 3 * rows, (width + 2) * rows, 16, rows)
    sweep(a0, d0, s0, g0, modes, own0, size0, 16, rows)
    finish()


def coupling_places(coupling_list, mode, modes):
    side = mode % 2
    targets = jnp.concatenate([
        mode * modes + jnp.arange(modes, dtype=jnp.int32),
        (mode + 1 - 2 * side) * modes + jnp.arange(modes, dtype=jnp.int32),
    ])
    wanted = (targets[:, None] * 8 + jnp.arange(1, KL + 1, dtype=jnp.int32)[None, :]).reshape(-1)
    given = coupling_list[0] * 8 + coupling_list[2]
    other = coupling_list[1]
    held = (other // modes) % 2 == side
    slot = other // (2 * modes) * modes + other % modes
    match = jnp.logical_and(wanted[:, None] == given[None, :], held[None, :])
    code = jnp.where(match, slot * 4 + coupling_list[3], -1)
    high = jnp.max(code, axis=1)
    low = jnp.min(jnp.where(match, slot * 4 + coupling_list[3], 1 << 20), axis=1)
    low = jnp.where(low < high, low, 0)
    both = jnp.maximum(jnp.stack([high, low]), 0)
    return both // 4, jnp.sqrt((both % 4).astype(F32))


def local(blocks, pressure, source, kl_field, coupling_list):
    modes, width, rows, depth = pressure.shape
    plane = width * rows
    even = modes + modes % 2
    r1, r2, r3 = rows // 2, rows // 4, rows // 8
    grid = width * blocks
    n0 = (width + 8) * rows + 2 * PAD
    n1 = (width // 2 + 10) * r1 + 2 * PAD
    n2 = (width // 4 + 12) * r2 + 2 * PAD
    n3 = grid // 8 * r3 + 2 * PAD
    scratch = []
    for size, count in ((n0, even), (n1, even // 2), (n2, even // 4), (n3, 1)):
        scratch += [pltpu.VMEM((size, LANES), F32)] * 3
        scratch += [pltpu.VMEM((6, size, LANES), F32)]
        scratch += [pltpu.VMEM((count, size, LANES), F32)] * 4
    held = RING * modes
    scratch += [
        pltpu.VMEM((512, LANES), F32),
        pltpu.VMEM((3, grid // 8, LANES), F32),
        pltpu.VMEM((grid // 8, LANES), F32),
        pltpu.VMEM((24, LANES), F32),
        pltpu.VMEM((2, ROW, 8, LANES), F32),
    ]
    scratch += [pltpu.VMEM((held, count * rows, LANES), F32) for _, count in CHUNKS]
    scratch += [pltpu.VMEM((held, rows, LANES), F32)] * 2
    scratch += [pltpu.VMEM((KL, (width + 2) * rows + 2 * PAD, LANES), F32)]
    scratch += [pltpu.VMEM((KL + 1, (width + 1) * rows, LANES), F32)] * 3
    scratch += [pltpu.VMEM((modes * KL, rows + 8, LANES), F32)] * 4
    scratch += [pltpu.VMEM((modes * (KL + 1), rows + 8, LANES), F32)] * 2
    scratch += [pltpu.VMEM((modes, rows, LANES), F32)] * 3
    scratch += [pltpu.VMEM((width, modes, rows, LANES), F32)] * 2
    scratch += [pltpu.SemaphoreType.DMA((COPIES,))] * 2
    geometry = (modes, width, rows, blocks)
    places, shares = coupling_places(coupling_list, lax.axis_index("mode"), modes)
    shape = jax.ShapeDtypeStruct((modes, plane, depth), F32)
    out, residual = pl.pallas_call(
        lambda *refs: cycle_kernel(geometry, *refs),
        out_shape=(shape, shape),
        in_specs=[pl.BlockSpec(memory_space=pltpu.SMEM)] * 2 + [pl.BlockSpec(memory_space=pltpu.VMEM)] * 3,
        out_specs=[pl.BlockSpec(memory_space=pltpu.VMEM)] * 2,
        scratch_shapes=scratch,
        compiler_params=pltpu.CompilerParams(
            collective_id=1, has_side_effects=True, vmem_limit_bytes=60 * 2**20),
        name="coupled_cycle",
    )(places, shares, pressure.reshape(modes, plane, depth), source.reshape(modes, plane, depth),
      kl_field.reshape(KL + 1, plane, depth))
    return (out.reshape(pressure.shape), residual.reshape(pressure.shape))


def solution(mesh):
    in_specs = (
        P("mode", "space", None, None),
        P("mode", "space", None, None),
        P(None, "space", None, None),
        P(),
    )
    out_specs = (P("mode", "space", None, None), P("mode", "space", None, None))
    blocks = mesh.shape["space"]
    return jax.shard_map(lambda *arrays: local(blocks, *arrays), mesh=mesh, in_specs=in_specs, out_specs=out_specs, check_vma=False)
```

```python
import jax
import jax.numpy as jnp
from jax import lax
from jax.sharding import PartitionSpec as P
from jax.experimental import pallas as pl
from jax.experimental.pallas import tpu as pltpu

MESH = pl.DeviceIdType.MESH
F32 = jnp.float32
P_SIZE = 56
KL = 5
RING = 4
CHUNKS = ((7, 1), (0, 1), (1, 1), (2, 1), (6, 1), (5, 1), (3, 1), (4, 1))
COPIES = 96
NEAR = (1, -1, 2, -2, 3, -3)
SWEEPS = 2
COARSE = 8
LEVELS = 4
LANES = 128
ROW = 8
COLS = 4
PAD = 16


def split_dot(values, matrix):
    high = values.astype(jnp.bfloat16)
    low = (values - high.astype(F32)).astype(jnp.bfloat16)
    return jnp.dot(high, matrix, preferred_element_type=F32) + jnp.dot(
        low, matrix, preferred_element_type=F32
    )


def pairing():
    wide = lax.broadcasted_iota(jnp.int32, (2 * LANES, LANES), 0)
    narrow = lax.broadcasted_iota(jnp.int32, (2 * LANES, LANES), 1)
    return jnp.where(wide // 2 == narrow, 1.0, 0.0).astype(jnp.bfloat16)


def spreading():
    narrow = lax.broadcasted_iota(jnp.int32, (LANES, 2 * LANES), 0)
    wide = lax.broadcasted_iota(jnp.int32, (LANES, 2 * LANES), 1)
    return jnp.where(wide // 2 == narrow, 1.0, 0.0).astype(jnp.bfloat16)


def level_faces(coef, faces, weight, inverse, first, count, step, rows, depth, scale, origin, width):
    bits = rows.bit_length() - 1
    lane = lax.broadcasted_iota(jnp.int32, (step, LANES), 1) & (depth - 1)
    place = lax.broadcasted_iota(jnp.int32, (step, LANES), 0)

    @pl.loop(0, count // step)
    def _(turn):
        base = pl.multiple_of(first + turn * step, 8)
        at = place + (base - PAD)
        y = at & (rows - 1)
        x = (at >> bits) + origin
        inside = jnp.logical_and(x >= 0, x < width)
        c = coef[pl.ds(base, step), :]
        others = (
            (coef[pl.ds(base + rows, step), :], None),
            (coef[pl.ds(base - rows, step), :], None),
            (coef[pl.ds(base + 1, step), :], y < rows - 1),
            (coef[pl.ds(base - 1, step), :], y > 0),
            (pltpu.roll(c, LANES - 1, 1), lane < depth - 1),
            (pltpu.roll(c, 1, 1), lane > 0),
        )
        sides = []
        total = jnp.zeros_like(c)
        for other, keep in others:
            face = 0.5 * (c + other)
            if keep is not None:
                face = jnp.where(keep, face, 0.0)
            sides.append(face)
            total = total + face
        part = jnp.where(inside, 0.8 / jnp.where(inside, total, 1.0), 0.0)
        weight[pl.ds(base, step), :] = part * (1.0 / scale)
        inverse[pl.ds(base, step), :] = jnp.where(inside, total * (scale * 1.25), 0.0)
        for n in range(6):
            faces[n, pl.ds(base, step), :] = part * sides[n]


def first_sweep(start, right, weight, modes, first, count, step):
    @pl.loop(0, count // step)
    def _(turn):
        base = pl.multiple_of(first + turn * step, 8)
        w = weight[pl.ds(base, step), :]
        for m in range(modes):
            start[m, pl.ds(base, step), :] = w * right[m, pl.ds(base, step), :]


def sweep(out, now, start, faces, modes, first, count, step, rows, keep=0.2, inverse=None):
    @pl.loop(0, count // step)
    def _(turn):
        base = pl.multiple_of(first + turn * step, 8)
        g = [faces[n, pl.ds(base, step), :] for n in range(6)]
        for m in range(modes):
            c = now[m, pl.ds(base, step), :]
            total = start[m, pl.ds(base, step), :] + (keep if inverse is None else -0.8) * c
            total = total + g[0] * now[m, pl.ds(base + rows, step), :]
            total = total + g[1] * now[m, pl.ds(base - rows, step), :]
            total = total + g[2] * now[m, pl.ds(base + 1, step), :]
            total = total + g[3] * now[m, pl.ds(base - 1, step), :]
            total = total + g[4] * pltpu.roll(c, LANES - 1, 1)
            total = total + g[5] * pltpu.roll(c, 1, 1)
            if inverse is not None:
                total = total * inverse[pl.ds(base, step), :]
            out[m, pl.ds(base, step), :] = total


def pair_xy(values, first, planes, rows, temp):
    for x in range(planes // 2):
        temp[pl.ds(x * rows, rows), :] = (
            values[pl.ds(first + 2 * x * rows, rows), :]
            + values[pl.ds(first + (2 * x + 1) * rows, rows), :]
        )
    half = planes // 2 * rows // 2
    return temp[pl.ds(0, half, 2), :] + temp[pl.ds(1, half, 2), :]


def restrict_pair(left, right, matrix):
    return 0.125 * split_dot(jnp.concatenate([left, right], axis=-1), matrix)


def prolong(fine, modes, fine_first, coarse, planes, rows, matrix, temp):
    count = planes * rows
    for p in range((modes + 1) // 2):
        both = split_dot(coarse(p), matrix)
        for part in range(2):
            m = 2 * p + part
            if m >= modes:
                continue
            child = both[:, part * LANES : (part + 1) * LANES]
            temp[pl.ds(0, count, 2), :] = child
            temp[pl.ds(1, count, 2), :] = child
            for x in range(planes):
                child_plane = temp[pl.ds(2 * x * rows, 2 * rows), :]
                for side in range(2):
                    at = pl.ds(fine_first + (2 * x + side) * 2 * rows, 2 * rows)
                    fine[m, at, :] = fine[m, at, :] + child_plane


def zero_all(ref):
    ref[...] = jnp.zeros(ref.shape, ref.dtype)


def cycle_kernel(
    geometry, place_ref, share_ref, p_ref, source_ref, field_ref, out_ref, residual_ref,
    c0, w0, i0, g0, b0, s0, a0, d0,
    c1, w1, i1, g1, b1, s1, a1, d1,
    c2, w2, i2, g2, b2, s2, a2, d2,
    c3, w3, i3, g3, b3, s3, a3, d3,
    temp, line, sums,
    small, slots, q0, q1, q2, q3, q4, q5, q6, q7, rim_low, rim_high, spread_fields, face_x, face_y, face_z,
    mix_a, mix_b, mix_c, mix_d, mix_e, mix_f, hold_a, hold_b, hold_c, partial, arriving,
    send_sem, recv_sem,
):
    modes, width, rows, blocks = geometry
    grid = width * blocks
    me = lax.axis_index("space")
    mode = lax.axis_index("mode")
    r1, r2, r3 = rows // 2, rows // 4, rows // 8
    n1, n2 = width // 2, width // 4
    row_at, col_at = me % ROW, me // ROW
    cols = blocks // ROW
    counter = [0]

    def start_copy(src, dst, target, exists=None, other_mode=None):
        number = counter[0]
        counter[0] += 1
        copy = pltpu.make_async_remote_copy(
            src_ref=src, dst_ref=dst, send_sem=send_sem.at[number], recv_sem=recv_sem.at[number],
            device_id=(target, mode if other_mode is None else other_mode), device_id_type=MESH,
        )
        if exists is None:
            copy.start()
        else:
            pl.when(exists)(copy.start)
        return copy

    def finish():
        for m in range(modes):
            out_ref[m] = a0[m, pl.ds(own0, size0), :]
        for copy, exists in sends:
            if exists is None:
                copy.wait_send()
            else:
                pl.when(exists)(copy.wait_send)

    def shift_exists(delta):
        return me + delta < blocks if delta > 0 else me + delta >= 0

    sends = []

    def to_neighbour(src, dst, delta):
        copy = start_copy(src, dst, me + delta, shift_exists(delta))
        sends.append((copy, shift_exists(delta)))
        return (copy, shift_exists(-delta))

    def arrived(pair):
        copy, exists = pair
        if exists is None:
            copy.wait_recv()
        else:
            pl.when(exists)(copy.wait_recv)

    def row_peer(q):
        return col_at * ROW + (row_at + q) % ROW

    def col_peer(q):
        return ((col_at + q) % cols) * ROW + row_at

    own0 = PAD + 4 * rows
    size0 = width * rows
    for ref in (c0, c1, b1, c2, b2, c3):
        zero_all(ref)
    for at in (pl.ds(own0 - 3 * rows, 3 * rows), pl.ds(own0 + size0, 3 * rows)):
        b0[:, at, :] = jnp.zeros((b0.shape[0], 3 * rows, LANES), F32)
    spread_fields[...] = jnp.zeros(spread_fields.shape, F32)

    @pl.when(me == 0)
    def _():
        zero_all(rim_low)

    @pl.when(me == blocks - 1)
    def _():
        zero_all(rim_high)

    barrier = pltpu.get_barrier_semaphore()
    expected = ROW - 1 + cols - 1
    for delta in NEAR:
        @pl.when(shift_exists(delta))
        def _():
            pl.semaphore_signal(barrier, inc=1, device_id=(me + delta, mode), device_id_type=MESH)
        expected = expected + jnp.where(shift_exists(delta), 1, 0)
    for q in range(1, ROW):
        pl.semaphore_signal(barrier, inc=1, device_id=(row_peer(q), mode), device_id_type=MESH)
    for q in range(1, cols):
        pl.semaphore_signal(barrier, inc=1, device_id=(col_peer(q), mode), device_id_type=MESH)
    y = mode // 2
    partner = y * 2 + 1 - mode % 2
    up, down = (mode + 2) % (2 * RING), (mode + 2 * RING - 2) % (2 * RING)
    for other in (up, down, partner):
        pl.semaphore_signal(barrier, inc=1, device_id=(me, other), device_id_type=MESH)
    expected = expected + 3
    own_slot = pl.ds(y * modes, modes)
    parts = (q0, q1, q2, q3, q4, q5, q6, q7)
    for (plane, count), part in zip(CHUNKS, parts):
        for m in range(modes):
            part[y * modes + m] = p_ref[m, pl.ds(plane * rows, count * rows), :]
    pl.semaphore_wait(barrier, expected)

    def slot(distance, first=0, count=modes):
        return pl.ds((y + RING + distance) % RING * modes + first, count)

    near, far = {}, {}

    def send_own(c):
        plane, count = CHUNKS[c]
        src = p_ref.at[:, pl.ds(plane * rows, count * rows)]
        dst = parts[c].at[own_slot]
        near[c] = (start_copy(src, dst, me, None, up), start_copy(src, dst, me, None, down))
        sends.extend((copy, None) for copy in near[c])

    def pass_on(c):
        cut = modes // 2 + (c + 1) % 2
        near[c][0].wait_recv()
        at = parts[c].at[slot(-1, 0, cut)]
        first = start_copy(at, at, me, None, up)
        near[c][1].wait_recv()
        at = parts[c].at[slot(1, cut, modes - cut)]
        far[c] = (first, start_copy(at, at, me, None, down))
        sends.extend((copy, None) for copy in far[c])

    def complete(c):
        far[c][0].wait_recv()
        far[c][1].wait_recv()

    send_own(0)
    send_own(1)

    c_halos = []
    c_halos.append(to_neighbour(field_ref.at[0, pl.ds(size0 - 4 * rows, 4 * rows)], c0.at[pl.ds(own0 - 4 * rows, 4 * rows)], 1))
    c_halos.append(to_neighbour(field_ref.at[0, pl.ds(0, 4 * rows)], c0.at[pl.ds(own0 + size0, 4 * rows)], -1))
    own_f = PAD + rows
    c_halos.append(to_neighbour(field_ref.at[pl.ds(1, KL), pl.ds(size0 - rows, rows)], spread_fields.at[:, pl.ds(PAD, rows)], 1))
    c_halos.append(to_neighbour(field_ref.at[pl.ds(1, KL), pl.ds(0, rows)], spread_fields.at[:, pl.ds(own_f + size0, rows)], -1))
    c0[pl.ds(own0, size0), :] = field_ref[0]
    for k in range(KL):
        spread_fields[k, pl.ds(own_f, size0), :] = field_ref[k + 1]
    for mix in (mix_a, mix_b, mix_c, mix_d, mix_e, mix_f):
        mix[:, pl.ds(rows, 8), :] = jnp.zeros((mix.shape[0], 8, LANES), F32)
    def all_faces():
        for pair in c_halos:
            arrived(pair)

        @pl.loop(0, width + 1)
        def _(turn):
            lane = lax.broadcasted_iota(jnp.int32, (rows, LANES), 1)
            line_at = lax.broadcasted_iota(jnp.int32, (rows, LANES), 0)
            base = pl.multiple_of(turn * rows, 8)
            for k in range(KL + 1):
                ref = c0 if k == 0 else spread_fields.at[k - 1]
                shift = own0 - rows if k == 0 else PAD
                here = ref[pl.ds(shift + base, rows), :]
                face_x[k, pl.ds(base, rows), :] = 0.5 * (here + ref[pl.ds(shift + base + rows, rows), :])
                face_y[k, pl.ds(base, rows), :] = jnp.where(
                    line_at < rows - 1, 0.5 * (here + ref[pl.ds(shift + base + 1, rows), :]), 0.0)
                face_z[k, pl.ds(base, rows), :] = jnp.where(
                    lane < LANES - 1, 0.5 * (here + pltpu.roll(here, LANES - 1, 1)), 0.0)

    def source_of(x):
        if x < 0:
            return rim_low, 0
        if x >= width:
            return rim_high, 0
        for (plane, count), part in zip(CHUNKS, parts):
            if plane <= x < plane + count:
                return part, (x - plane) * rows

    def mixed(t, k, x):
        ref, at = source_of(x)
        entry = t * KL + k
        return (
            share_ref[0, entry] * ref[place_ref[0, entry], pl.ds(at, rows), :]
            + share_ref[1, entry] * ref[place_ref[1, entry], pl.ds(at, rows), :]
        )

    def fill(first, fields, now, x):
        @pl.loop(0, modes)
        def _(t):
            for k in range(KL):
                now[t * fields + k, pl.ds(0, rows), :] = mixed(first + t, k, x)
            if fields > KL:
                ref, at = source_of(x)
                now[t * fields + KL, pl.ds(0, rows), :] = ref[y * modes + t, pl.ds(at, rows), :]

    def advance(first, fields, now, later, hold, x, emit):
        here = pl.ds((x + 1) * rows, rows)

        @pl.loop(0, modes)
        def _(t):
            along_x = jnp.zeros((rows, LANES), F32)
            along_y, along_z = along_x, along_x
            for k in range(fields):
                if k < KL:
                    field = k + 1
                    value = mixed(first + t, k, x + 1)
                else:
                    field = 0
                    ref, at = source_of(x + 1)
                    value = ref[y * modes + t, pl.ds(at, rows), :]
                at = t * fields + k
                later[at, pl.ds(0, rows), :] = value
                old = now[at, pl.ds(0, rows), :]
                along_x = along_x + face_x[field, here, :] * (old - value)
                if emit is not None:
                    along_y = along_y + face_y[field, here, :] * (old - now[at, pl.ds(1, rows), :])
                    along_z = along_z + face_z[field, here, :] * (old - pltpu.roll(old, LANES - 1, 1))
            if emit is not None:
                emit(t, along_x - hold[t] + (along_y - pltpu.roll(along_y, 1, 0))
                     + (along_z - pltpu.roll(along_z, 1, 1)))
            hold[t] = along_x

    to_partner = {}

    def send_partner(x):
        to_partner[x] = start_copy(partial.at[x], arriving.at[x], me, None, partner)
        sends.append((to_partner[x], None))

    def emit_partner(x):
        def emit(t, value):
            partial[x, t] = value
        return emit

    def emit_own(x):
        def emit(t, value):
            at = pl.ds(own0 + x * rows, rows)
            b0[t, at, :] = source_ref[t, pl.ds(x * rows, rows), :] - value
        return emit

    def partner_step(now, later, hold, x, emits=True):
        advance(modes, KL, now, later, hold, x, emit_partner(x) if emits else None)

    merge = pairing()
    spread = spreading()
    own1 = PAD + 5 * r1
    size1 = n1 * r1
    own2 = PAD + 6 * r2
    size2 = n2 * r2
    columns = grid // 8
    all3 = columns * r3

    def gather_small(value, dest, turn):
        slots[turn, row_at, pl.ds(0, r3), :] = value
        copies = []
        for q in range(1, ROW):
            copy = start_copy(slots.at[turn, row_at], slots.at[turn, row_at], row_peer(q))
            sends.append((copy, None))
            copies.append((copy, None))

        def second():
            for pair in copies:
                arrived(pair)
            first = pl.multiple_of(PAD + col_at * (ROW * r3), 8)
            for n in range(0, ROW, 2):
                dest[pl.ds(first + n * r3, 2 * r3), :] = jnp.concatenate(
                    [slots[turn, n, pl.ds(0, r3), :], slots[turn, n + 1, pl.ds(0, r3), :]], axis=0)
            at = pl.ds(first, ROW * r3)
            more = []
            for q in range(1, cols):
                copy = start_copy(dest.at[at], dest.at[at], col_peer(q))
                sends.append((copy, None))
                more.append((copy, None))
            return more

        return second

    def coarse_coefficients():
        part = pair_xy(c0, own0, width, rows, temp)
        c1[pl.ds(own1, size1), :] = restrict_pair(part, part, merge)
        found = [
            to_neighbour(c1.at[pl.ds(own1, size1)], c1.at[pl.ds(own1 - size1, size1)], 1),
            to_neighbour(c1.at[pl.ds(own1, size1)], c1.at[pl.ds(own1 + size1, size1)], -1),
            to_neighbour(c1.at[pl.ds(own1 + size1 - r1, r1)], c1.at[pl.ds(own1 - size1 - r1, r1)], 2),
            to_neighbour(c1.at[pl.ds(own1, r1)], c1.at[pl.ds(own1 + 2 * size1, r1)], -2),
        ]
        part = pair_xy(c1, own1, n1, r1, temp)
        c2[pl.ds(own2, size2), :] = restrict_pair(part, part, merge)
        for delta in NEAR:
            found.append(to_neighbour(c2.at[pl.ds(own2, size2)], c2.at[pl.ds(own2 - delta * size2, size2)], delta))
        part = pair_xy(c2, own2, n2, r2, temp)
        return found, gather_small(restrict_pair(part, part, merge), c3, 0)

    def column_sums(values):
        gather = jnp.where(
            lax.broadcasted_iota(jnp.int32, (columns, all3), 1) // r3
            == lax.broadcasted_iota(jnp.int32, (columns, all3), 0), 1.0, 0.0)
        within = jnp.where(
            lax.broadcasted_iota(jnp.int32, (LANES, LANES), 1) // (LANES // 8)
            == lax.broadcasted_iota(jnp.int32, (LANES, LANES), 0) // (LANES // 8), 1.0, 0.0)
        return jnp.dot(
            jnp.dot(gather, values, precision=lax.Precision.HIGHEST, preferred_element_type=F32),
            within, precision=lax.Precision.HIGHEST, preferred_element_type=F32)

    def line_factors():
        diag3 = i3[pl.ds(PAD, all3), :]
        line[0] = column_sums(g3[1, pl.ds(PAD, all3), :] * diag3)
        line[2] = column_sums(g3[0, pl.ds(PAD, all3), :] * diag3)
        ratio = None
        for x in range(columns):
            low, high = line[0, pl.ds(x, 1), :], line[2, pl.ds(x, 1), :]
            den = low + high
            if ratio is not None:
                den = den - low * ratio
            inv = 1.0 / den
            ratio = high * inv
            line[0, pl.ds(x, 1), :] = low * inv
            line[1, pl.ds(x, 1), :] = inv
            line[2, pl.ds(x, 1), :] = ratio

    all_faces()
    pass_on(0)
    send_own(2)
    coarse_halos, coarse_second = coarse_coefficients()
    pass_on(1)
    send_own(3)
    complete(0)
    low = to_neighbour(q0, rim_low, 1)
    for ref in (s3, a3, d3):
        zero_all(ref)
    pass_on(2)
    send_own(4)
    complete(1)
    high = to_neighbour(q1, rim_high, -1)
    for ref in (s2, a2, d2, s1, a1, d1):
        zero_all(ref)
    pass_on(3)
    send_own(5)
    complete(2)
    arrived(low)
    fill(modes, KL, mix_a, -1)
    partner_step(mix_a, mix_b, hold_a, -1, False)
    partner_step(mix_b, mix_a, hold_a, 0)
    send_partner(0)
    pass_on(4)
    send_own(6)
    c3_more = coarse_second()
    complete(3)
    partner_step(mix_a, mix_b, hold_a, 1)
    send_partner(1)
    pass_on(5)
    send_own(7)
    for pair in coarse_halos:
        arrived(pair)
    level_faces(c1, g1, w1, i1, PAD + r1, (n1 + 8) * r1, 16, r1, LANES // 2, 0.25, me * n1 - 5, grid // 2)
    level_faces(c2, g2, w2, i2, PAD + r2, (n2 + 10) * r2, 16, r2, LANES // 4, 0.0625, me * n2 - 6, grid // 4)
    pass_on(6)
    complete(4)
    complete(5)
    arrived(high)
    fill(modes, KL, mix_c, 5)
    partner_step(mix_c, mix_d, hold_b, 5, False)
    partner_step(mix_d, mix_c, hold_b, 6)
    send_partner(6)
    pass_on(7)
    partner_step(mix_c, mix_d, hold_b, 7)
    send_partner(7)
    complete(6)
    partner_step(mix_b, mix_a, hold_a, 2)
    send_partner(2)
    complete(7)
    partner_step(mix_a, mix_b, hold_a, 3)
    partner_step(mix_b, mix_a, hold_a, 4)
    partner_step(mix_a, mix_b, hold_a, 5)
    send_partner(5)
    fill(0, KL + 1, mix_e, -1)
    now, later = mix_e, mix_f
    for x in range(-1, width):
        advance(0, KL + 1, now, later, hold_c, x, emit_own(x) if x >= 0 else None)
        now, later = later, now
        if x == 1:
            send_partner(3)
            send_partner(4)
    level_faces(c0, g0, w0, i0, PAD + rows, (width + 6) * rows, 16, rows, LANES, 1.0, me * width - 4, grid)
    for pair in c3_more:
        arrived(pair)
    level_faces(c3, g3, w3, i3, PAD, all3, 32, r3, LANES // 8, 0.015625, 0, grid // 8)
    line_factors()
    for ref in (s0, a0, d0):
        zero_all(ref)

    def receive(x):
        to_partner[x].wait_recv()
        at = pl.ds(own0 + x * rows, rows)
        for m in range(modes):
            value = b0[m, at, :] - arriving[x, m]
            b0[m, at, :] = value
            residual_ref[m, pl.ds(x * rows, rows), :] = value

    halos = []
    for x in (0, 1, 2):
        receive(x)
    halos.append(to_neighbour(b0.at[pl.ds(0, modes), pl.ds(own0, 3 * rows)], b0.at[pl.ds(0, modes), pl.ds(own0 + size0, 3 * rows)], -1))
    for x in (6, 7, 5):
        receive(x)
    halos.append(to_neighbour(b0.at[pl.ds(0, modes), pl.ds(own0 + size0 - 3 * rows, 3 * rows)], b0.at[pl.ds(0, modes), pl.ds(own0 - 3 * rows, 3 * rows)], 1))
    for x in (3, 4):
        receive(x)
    first_sweep(s0, b0, w0, modes, own0, size0, 32)
    sweep(a0, s0, s0, g0, modes, own0 + rows, size0 - 2 * rows, 32, rows)
    for pair in halos:
        arrived(pair)
    for at in (own0 - 3 * rows, own0 + size0):
        first_sweep(s0, b0, w0, modes, at, 3 * rows, 32)
    for at in (own0 - 2 * rows, own0 + size0 - rows):
        sweep(a0, s0, s0, g0, modes, at, 3 * rows, 32, rows)
    sweep(d0, a0, s0, g0, modes, own0, size0, 32, rows, inverse=i0)
    pairs1 = b1.shape[0]
    for p in range(pairs1):
        left = pair_xy(d0.at[2 * p], own0, width, rows, temp)
        right = pair_xy(d0.at[2 * p + 1], own0, width, rows, temp)
        b1[p, pl.ds(own1, size1), :] = restrict_pair(left, right, merge)
    b1_halos = [
        to_neighbour(b1.at[:, pl.ds(own1, size1)], b1.at[:, pl.ds(own1 - size1, size1)], 1),
        to_neighbour(b1.at[:, pl.ds(own1, size1)], b1.at[:, pl.ds(own1 + size1, size1)], -1),
    ]
    for pair in b1_halos:
        arrived(pair)
    first_sweep(s1, b1, w1, pairs1, PAD + r1, (n1 + 8) * r1, 32)
    sweep(a1, s1, s1, g1, pairs1, PAD + 2 * r1, (n1 + 6) * r1, 32, r1)
    sweep(d1, a1, s1, g1, pairs1, own1, size1, 32, r1, inverse=i1)
    pairs2 = b2.shape[0]
    for p in range(pairs2):
        left = pair_xy(d1.at[2 * p], own1, n1, r1, temp)
        right = pair_xy(d1.at[2 * p + 1], own1, n1, r1, temp)
        b2[p, pl.ds(own2, size2), :] = restrict_pair(left, right, merge)
    b2_halos = []
    for delta in NEAR:
        b2_halos.append(to_neighbour(b2.at[:, pl.ds(own2, size2)], b2.at[:, pl.ds(own2 - delta * size2, size2)], delta))
    for pair in b2_halos:
        arrived(pair)
    first_sweep(s2, b2, w2, pairs2, PAD + r2, (n2 + 10) * r2, 48)
    sweep(a2, s2, s2, g2, pairs2, PAD + 2 * r2, (n2 + 8) * r2, 40, r2)
    sweep(d2, a2, s2, g2, pairs2, own2, size2, 16, r2, inverse=i2)
    left = pair_xy(d2.at[0], own2, n2, r2, temp)
    right = pair_xy(d2.at[1], own2, n2, r2, temp)
    second = gather_small(restrict_pair(left, right, merge), b3.at[0], 1)
    for pair in second():
        arrived(pair)
    first_sweep(s3, b3, w3, 1, PAD, all3, all3)
    now, other = s3, a3
    for turn in range(COARSE - 1):
        sweep(other, now, s3, g3, 1, PAD, all3, all3, r3)
        now, other = (a3, d3) if now is s3 else (other, now)
    sweep(other, now, s3, g3, 1, PAD, all3, all3, r3, inverse=i3)
    sums[...] = column_sums(other[0, pl.ds(PAD, all3), :])
    carried = None
    for x in range(columns):
        value = sums[pl.ds(x, 1), :] * line[1, pl.ds(x, 1), :]
        if carried is not None:
            value = value + line[0, pl.ds(x, 1), :] * carried
        sums[pl.ds(x, 1), :] = value
        carried = value
    carried = None
    for x in reversed(range(columns)):
        value = sums[pl.ds(x, 1), :]
        if carried is not None:
            value = value + line[2, pl.ds(x, 1), :] * carried
        carried = value
        at = pl.ds(PAD + x * r3, r3)
        now[0, at, :] = now[0, at, :] + jnp.broadcast_to(value, (r3, LANES))
    for x in range(5):
        small[pl.ds(x * r3, r3), :] = now[0, pl.ds(PAD + (me + x - 2) * r3, r3), :]
    prolong(a2, pairs2, PAD + 2 * r2, lambda p: small[pl.ds(0, 5 * r3), :], 5, r3, spread, temp)
    sweep(d2, a2, s2, g2, pairs2, PAD + 3 * r2, (n2 + 6) * r2, 32, r2)
    sweep(a2, d2, s2, g2, pairs2, PAD + 4 * r2, (n2 + 4) * r2, 48, r2)
    prolong(a1, pairs1, PAD + r1, lambda p: a2[p, pl.ds(PAD + 4 * r2, (n2 + 4) * r2), :], n2 + 4, r2, spread, temp)
    sweep(d1, a1, s1, g1, pairs1, PAD + 3 * r1, (n1 + 4) * r1, 32, r1)
    sweep(a1, d1, s1, g1, pairs1, PAD + 4 * r1, (n1 + 2) * r1, 32, r1)
    prolong(a0, modes, PAD + 2 * rows, lambda p: a1[p, pl.ds(PAD + 4 * r1, (n1 + 2) * r1), :], n1 + 2, r1, spread, temp)
    sweep(d0, a0, s0, g0, modes, PAD + 3 * rows, (width + 2) * rows, 32, rows)
    sweep(a0, d0, s0, g0, modes, own0, size0, 32, rows)
    finish()


def coupling_places(coupling_list, mode, modes):
    side = mode % 2
    targets = jnp.concatenate([
        mode * modes + jnp.arange(modes, dtype=jnp.int32),
        (mode + 1 - 2 * side) * modes + jnp.arange(modes, dtype=jnp.int32),
    ])
    wanted = (targets[:, None] * 8 + jnp.arange(1, KL + 1, dtype=jnp.int32)[None, :]).reshape(-1)
    given = coupling_list[0] * 8 + coupling_list[2]
    other = coupling_list[1]
    held = (other // modes) % 2 == side
    slot = other // (2 * modes) * modes + other % modes
    match = jnp.logical_and(wanted[:, None] == given[None, :], held[None, :])
    code = jnp.where(match, slot * 4 + coupling_list[3], -1)
    high = jnp.max(code, axis=1)
    low = jnp.min(jnp.where(match, slot * 4 + coupling_list[3], 1 << 20), axis=1)
    low = jnp.where(low < high, low, 0)
    both = jnp.maximum(jnp.stack([high, low]), 0)
    return both // 4, jnp.sqrt((both % 4).astype(F32))


def local(blocks, pressure, source, kl_field, coupling_list):
    modes, width, rows, depth = pressure.shape
    plane = width * rows
    even = modes + modes % 2
    r1, r2, r3 = rows // 2, rows // 4, rows // 8
    grid = width * blocks
    n0 = (width + 8) * rows + 2 * PAD
    n1 = (width // 2 + 10) * r1 + 2 * PAD
    n2 = (width // 4 + 12) * r2 + 2 * PAD
    n3 = grid // 8 * r3 + 2 * PAD
    scratch = []
    for size, count in ((n0, even), (n1, even // 2), (n2, even // 4), (n3, 1)):
        scratch += [pltpu.VMEM((size, LANES), F32)] * 3
        scratch += [pltpu.VMEM((6, size, LANES), F32)]
        scratch += [pltpu.VMEM((count, size, LANES), F32)] * 4
    held = RING * modes
    scratch += [
        pltpu.VMEM((512, LANES), F32),
        pltpu.VMEM((3, grid // 8, LANES), F32),
        pltpu.VMEM((grid // 8, LANES), F32),
        pltpu.VMEM((24, LANES), F32),
        pltpu.VMEM((2, ROW, 8, LANES), F32),
    ]
    scratch += [pltpu.VMEM((held, count * rows, LANES), F32) for _, count in CHUNKS]
    scratch += [pltpu.VMEM((held, rows, LANES), F32)] * 2
    scratch += [pltpu.VMEM((KL, (width + 2) * rows + 2 * PAD, LANES), F32)]
    scratch += [pltpu.VMEM((KL + 1, (width + 1) * rows, LANES), F32)] * 3
    scratch += [pltpu.VMEM((modes * KL, rows + 8, LANES), F32)] * 4
    scratch += [pltpu.VMEM((modes * (KL + 1), rows + 8, LANES), F32)] * 2
    scratch += [pltpu.VMEM((modes, rows, LANES), F32)] * 3
    scratch += [pltpu.VMEM((width, modes, rows, LANES), F32)] * 2
    scratch += [pltpu.SemaphoreType.DMA((COPIES,))] * 2
    geometry = (modes, width, rows, blocks)
    places, shares = coupling_places(coupling_list, lax.axis_index("mode"), modes)
    shape = jax.ShapeDtypeStruct((modes, plane, depth), F32)
    out, residual = pl.pallas_call(
        lambda *refs: cycle_kernel(geometry, *refs),
        out_shape=(shape, shape),
        in_specs=[pl.BlockSpec(memory_space=pltpu.SMEM)] * 2 + [pl.BlockSpec(memory_space=pltpu.VMEM)] * 3,
        out_specs=[pl.BlockSpec(memory_space=pltpu.VMEM)] * 2,
        scratch_shapes=scratch,
        compiler_params=pltpu.CompilerParams(
            collective_id=1, has_side_effects=True, vmem_limit_bytes=60 * 2**20),
        name="coupled_cycle",
    )(places, shares, pressure.reshape(modes, plane, depth), source.reshape(modes, plane, depth),
      kl_field.reshape(KL + 1, plane, depth))
    return (out.reshape(pressure.shape), residual.reshape(pressure.shape))


def solution(mesh):
    in_specs = (
        P("mode", "space", None, None),
        P("mode", "space", None, None),
        P(None, "space", None, None),
        P(),
    )
    out_specs = (P("mode", "space", None, None), P("mode", "space", None, None))
    blocks = mesh.shape["space"]
    return jax.shard_map(lambda *arrays: local(blocks, *arrays), mesh=mesh, in_specs=in_specs, out_specs=out_specs, check_vma=False)
```

```python
import jax
import jax.numpy as jnp
from jax import lax
from jax.sharding import PartitionSpec as P
from jax.experimental import pallas as pl
from jax.experimental.pallas import tpu as pltpu

MESH = pl.DeviceIdType.MESH
F32 = jnp.float32
P_SIZE = 56
KL = 5
RING = 4
CHUNKS = ((7, 1), (0, 1), (1, 1), (2, 1), (6, 1), (5, 1), (3, 1), (4, 1))
COPIES = 96
NEAR = (1, -1, 2, -2, 3, -3)
SWEEPS = 2
COARSE = 8
LEVELS = 4
LANES = 128
ROW = 8
COLS = 4
PAD = 16


def split_dot(values, matrix):
    high = values.astype(jnp.bfloat16)
    low = (values - high.astype(F32)).astype(jnp.bfloat16)
    return jnp.dot(high, matrix, preferred_element_type=F32) + jnp.dot(
        low, matrix, preferred_element_type=F32
    )


def pairing():
    wide = lax.broadcasted_iota(jnp.int32, (2 * LANES, LANES), 0)
    narrow = lax.broadcasted_iota(jnp.int32, (2 * LANES, LANES), 1)
    return jnp.where(wide // 2 == narrow, 1.0, 0.0).astype(jnp.bfloat16)


def spreading():
    narrow = lax.broadcasted_iota(jnp.int32, (LANES, 2 * LANES), 0)
    wide = lax.broadcasted_iota(jnp.int32, (LANES, 2 * LANES), 1)
    return jnp.where(wide // 2 == narrow, 1.0, 0.0).astype(jnp.bfloat16)


def level_faces(coef, faces, weight, inverse, first, count, step, rows, depth, scale, origin, width):
    bits = rows.bit_length() - 1
    lane = lax.broadcasted_iota(jnp.int32, (step, LANES), 1) & (depth - 1)
    place = lax.broadcasted_iota(jnp.int32, (step, LANES), 0)

    @pl.loop(0, count // step)
    def _(turn):
        base = pl.multiple_of(first + turn * step, 8)
        at = place + (base - PAD)
        y = at & (rows - 1)
        x = (at >> bits) + origin
        inside = jnp.logical_and(x >= 0, x < width)
        c = coef[pl.ds(base, step), :]
        others = (
            (coef[pl.ds(base + rows, step), :], None),
            (coef[pl.ds(base - rows, step), :], None),
            (coef[pl.ds(base + 1, step), :], y < rows - 1),
            (coef[pl.ds(base - 1, step), :], y > 0),
            (pltpu.roll(c, LANES - 1, 1), lane < depth - 1),
            (pltpu.roll(c, 1, 1), lane > 0),
        )
        sides = []
        total = jnp.zeros_like(c)
        for other, keep in others:
            face = 0.5 * (c + other)
            if keep is not None:
                face = jnp.where(keep, face, 0.0)
            sides.append(face)
            total = total + face
        part = jnp.where(inside, 0.8 / jnp.where(inside, total, 1.0), 0.0)
        weight[pl.ds(base, step), :] = part * (1.0 / scale)
        inverse[pl.ds(base, step), :] = jnp.where(inside, total * (scale * 1.25), 0.0)
        for n in range(6):
            faces[n, pl.ds(base, step), :] = part * sides[n]


def first_sweep(start, right, weight, modes, first, count, step):
    @pl.loop(0, count // step)
    def _(turn):
        base = pl.multiple_of(first + turn * step, 8)
        w = weight[pl.ds(base, step), :]
        for m in range(modes):
            start[m, pl.ds(base, step), :] = w * right[m, pl.ds(base, step), :]


def sweep(out, now, start, faces, modes, first, count, step, rows, keep=0.2, inverse=None):
    @pl.loop(0, count // step)
    def _(turn):
        base = pl.multiple_of(first + turn * step, 8)
        g = [faces[n, pl.ds(base, step), :] for n in range(6)]
        for m in range(modes):
            c = now[m, pl.ds(base, step), :]
            total = start[m, pl.ds(base, step), :] + (keep if inverse is None else -0.8) * c
            total = total + g[0] * now[m, pl.ds(base + rows, step), :]
            total = total + g[1] * now[m, pl.ds(base - rows, step), :]
            total = total + g[2] * now[m, pl.ds(base + 1, step), :]
            total = total + g[3] * now[m, pl.ds(base - 1, step), :]
            total = total + g[4] * pltpu.roll(c, LANES - 1, 1)
            total = total + g[5] * pltpu.roll(c, 1, 1)
            if inverse is not None:
                total = total * inverse[pl.ds(base, step), :]
            out[m, pl.ds(base, step), :] = total


def pair_xy(values, first, planes, rows, temp):
    for x in range(planes // 2):
        temp[pl.ds(x * rows, rows), :] = (
            values[pl.ds(first + 2 * x * rows, rows), :]
            + values[pl.ds(first + (2 * x + 1) * rows, rows), :]
        )
    half = planes // 2 * rows // 2
    return temp[pl.ds(0, half, 2), :] + temp[pl.ds(1, half, 2), :]


def restrict_pair(left, right, matrix):
    return 0.125 * split_dot(jnp.concatenate([left, right], axis=-1), matrix)


def prolong(fine, modes, fine_first, coarse, planes, rows, matrix, temp):
    count = planes * rows
    for p in range((modes + 1) // 2):
        both = split_dot(coarse(p), matrix)
        for part in range(2):
            m = 2 * p + part
            if m >= modes:
                continue
            child = both[:, part * LANES : (part + 1) * LANES]
            temp[pl.ds(0, count, 2), :] = child
            temp[pl.ds(1, count, 2), :] = child
            for x in range(planes):
                child_plane = temp[pl.ds(2 * x * rows, 2 * rows), :]
                for side in range(2):
                    at = pl.ds(fine_first + (2 * x + side) * 2 * rows, 2 * rows)
                    fine[m, at, :] = fine[m, at, :] + child_plane


def zero_all(ref):
    ref[...] = jnp.zeros(ref.shape, ref.dtype)


def cycle_kernel(
    geometry, place_ref, share_ref, p_ref, source_ref, field_ref, out_ref, residual_ref,
    c0, w0, i0, g0, b0, s0, a0, d0,
    c1, w1, i1, g1, b1, s1, a1, d1,
    c2, w2, i2, g2, b2, s2, a2, d2,
    c3, w3, i3, g3, b3, s3, a3, d3,
    temp, line, sums,
    small, slots, q0, q1, q2, q3, q4, q5, q6, q7, rim_low, rim_high, spread_fields, face_x, face_y, face_z,
    mix_a, mix_b, mix_c, mix_d, mix_e, mix_f, hold_a, hold_b, hold_c, partial, arriving,
    send_sem, recv_sem,
):
    modes, width, rows, blocks = geometry
    grid = width * blocks
    me = lax.axis_index("space")
    mode = lax.axis_index("mode")
    r1, r2, r3 = rows // 2, rows // 4, rows // 8
    n1, n2 = width // 2, width // 4
    row_at, col_at = me % ROW, me // ROW
    cols = blocks // ROW
    counter = [0]

    def start_copy(src, dst, target, exists=None, other_mode=None):
        number = counter[0]
        counter[0] += 1
        copy = pltpu.make_async_remote_copy(
            src_ref=src, dst_ref=dst, send_sem=send_sem.at[number], recv_sem=recv_sem.at[number],
            device_id=(target, mode if other_mode is None else other_mode), device_id_type=MESH,
        )
        if exists is None:
            copy.start()
        else:
            pl.when(exists)(copy.start)
        return copy

    def finish():
        for m in range(modes):
            out_ref[m] = a0[m, pl.ds(own0, size0), :]
        for copy, exists in sends:
            if exists is None:
                copy.wait_send()
            else:
                pl.when(exists)(copy.wait_send)

    def shift_exists(delta):
        return me + delta < blocks if delta > 0 else me + delta >= 0

    sends = []

    def to_neighbour(src, dst, delta):
        copy = start_copy(src, dst, me + delta, shift_exists(delta))
        sends.append((copy, shift_exists(delta)))
        return (copy, shift_exists(-delta))

    def arrived(pair):
        copy, exists = pair
        if exists is None:
            copy.wait_recv()
        else:
            pl.when(exists)(copy.wait_recv)

    def row_peer(q):
        return col_at * ROW + (row_at + q) % ROW

    def col_peer(q):
        return ((col_at + q) % cols) * ROW + row_at

    own0 = PAD + 4 * rows
    size0 = width * rows
    for ref in (c0, c1, b1, c2, b2, c3):
        zero_all(ref)
    for at in (pl.ds(own0 - 3 * rows, 3 * rows), pl.ds(own0 + size0, 3 * rows)):
        b0[:, at, :] = jnp.zeros((b0.shape[0], 3 * rows, LANES), F32)
    spread_fields[...] = jnp.zeros(spread_fields.shape, F32)

    @pl.when(me == 0)
    def _():
        zero_all(rim_low)

    @pl.when(me == blocks - 1)
    def _():
        zero_all(rim_high)

    barrier = pltpu.get_barrier_semaphore()
    expected = ROW - 1 + cols - 1
    for delta in NEAR:
        @pl.when(shift_exists(delta))
        def _():
            pl.semaphore_signal(barrier, inc=1, device_id=(me + delta, mode), device_id_type=MESH)
        expected = expected + jnp.where(shift_exists(delta), 1, 0)
    for q in range(1, ROW):
        pl.semaphore_signal(barrier, inc=1, device_id=(row_peer(q), mode), device_id_type=MESH)
    for q in range(1, cols):
        pl.semaphore_signal(barrier, inc=1, device_id=(col_peer(q), mode), device_id_type=MESH)
    y = mode // 2
    partner = y * 2 + 1 - mode % 2
    up, down = (mode + 2) % (2 * RING), (mode + 2 * RING - 2) % (2 * RING)
    for other in (up, down, partner):
        pl.semaphore_signal(barrier, inc=1, device_id=(me, other), device_id_type=MESH)
    expected = expected + 3
    own_slot = pl.ds(y * modes, modes)
    parts = (q0, q1, q2, q3, q4, q5, q6, q7)
    for (plane, count), part in zip(CHUNKS, parts):
        for m in range(modes):
            part[y * modes + m] = p_ref[m, pl.ds(plane * rows, count * rows), :]
    pl.semaphore_wait(barrier, expected)

    def slot(distance, first=0, count=modes):
        return pl.ds((y + RING + distance) % RING * modes + first, count)

    near, far = {}, {}

    def send_own(c):
        plane, count = CHUNKS[c]
        src = p_ref.at[:, pl.ds(plane * rows, count * rows)]
        dst = parts[c].at[own_slot]
        near[c] = (start_copy(src, dst, me, None, up), start_copy(src, dst, me, None, down))
        sends.extend((copy, None) for copy in near[c])

    def pass_on(c):
        cut = modes // 2 + (c + 1) % 2
        near[c][0].wait_recv()
        at = parts[c].at[slot(-1, 0, cut)]
        first = start_copy(at, at, me, None, up)
        near[c][1].wait_recv()
        at = parts[c].at[slot(1, cut, modes - cut)]
        far[c] = (first, start_copy(at, at, me, None, down))
        sends.extend((copy, None) for copy in far[c])

    def complete(c):
        far[c][0].wait_recv()
        far[c][1].wait_recv()

    send_own(0)
    send_own(1)

    c_halos = []
    c_halos.append(to_neighbour(field_ref.at[0, pl.ds(size0 - 4 * rows, 4 * rows)], c0.at[pl.ds(own0 - 4 * rows, 4 * rows)], 1))
    c_halos.append(to_neighbour(field_ref.at[0, pl.ds(0, 4 * rows)], c0.at[pl.ds(own0 + size0, 4 * rows)], -1))
    own_f = PAD + rows
    c_halos.append(to_neighbour(field_ref.at[pl.ds(1, KL), pl.ds(size0 - rows, rows)], spread_fields.at[:, pl.ds(PAD, rows)], 1))
    c_halos.append(to_neighbour(field_ref.at[pl.ds(1, KL), pl.ds(0, rows)], spread_fields.at[:, pl.ds(own_f + size0, rows)], -1))
    c0[pl.ds(own0, size0), :] = field_ref[0]
    for k in range(KL):
        spread_fields[k, pl.ds(own_f, size0), :] = field_ref[k + 1]
    for mix in (mix_a, mix_b, mix_c, mix_d, mix_e, mix_f):
        mix[:, pl.ds(rows, 8), :] = jnp.zeros((mix.shape[0], 8, LANES), F32)
    def all_faces():
        for pair in c_halos:
            arrived(pair)

        @pl.loop(0, width + 1)
        def _(turn):
            lane = lax.broadcasted_iota(jnp.int32, (rows, LANES), 1)
            line_at = lax.broadcasted_iota(jnp.int32, (rows, LANES), 0)
            base = pl.multiple_of(turn * rows, 8)
            for k in range(KL + 1):
                ref = c0 if k == 0 else spread_fields.at[k - 1]
                shift = own0 - rows if k == 0 else PAD
                here = ref[pl.ds(shift + base, rows), :]
                face_x[k, pl.ds(base, rows), :] = 0.5 * (here + ref[pl.ds(shift + base + rows, rows), :])
                face_y[k, pl.ds(base, rows), :] = jnp.where(
                    line_at < rows - 1, 0.5 * (here + ref[pl.ds(shift + base + 1, rows), :]), 0.0)
                face_z[k, pl.ds(base, rows), :] = jnp.where(
                    lane < LANES - 1, 0.5 * (here + pltpu.roll(here, LANES - 1, 1)), 0.0)

    def source_of(x):
        if x < 0:
            return rim_low, 0
        if x >= width:
            return rim_high, 0
        for (plane, count), part in zip(CHUNKS, parts):
            if plane <= x < plane + count:
                return part, (x - plane) * rows

    def mixed(t, k, x):
        ref, at = source_of(x)
        entry = t * KL + k
        return (
            share_ref[0, entry] * ref[place_ref[0, entry], pl.ds(at, rows), :]
            + share_ref[1, entry] * ref[place_ref[1, entry], pl.ds(at, rows), :]
        )

    def fill(first, fields, now, x):
        @pl.loop(0, modes)
        def _(t):
            for k in range(KL):
                now[t * fields + k, pl.ds(0, rows), :] = mixed(first + t, k, x)
            if fields > KL:
                ref, at = source_of(x)
                now[t * fields + KL, pl.ds(0, rows), :] = ref[y * modes + t, pl.ds(at, rows), :]

    def advance(first, fields, now, later, hold, x, emit):
        here = pl.ds((x + 1) * rows, rows)

        @pl.loop(0, modes)
        def _(t):
            along_x = jnp.zeros((rows, LANES), F32)
            along_y, along_z = along_x, along_x
            for k in range(fields):
                if k < KL:
                    field = k + 1
                    value = mixed(first + t, k, x + 1)
                else:
                    field = 0
                    ref, at = source_of(x + 1)
                    value = ref[y * modes + t, pl.ds(at, rows), :]
                at = t * fields + k
                later[at, pl.ds(0, rows), :] = value
                old = now[at, pl.ds(0, rows), :]
                along_x = along_x + face_x[field, here, :] * (old - value)
                if emit is not None:
                    along_y = along_y + face_y[field, here, :] * (old - now[at, pl.ds(1, rows), :])
                    along_z = along_z + face_z[field, here, :] * (old - pltpu.roll(old, LANES - 1, 1))
            if emit is not None:
                emit(t, along_x - hold[t] + (along_y - pltpu.roll(along_y, 1, 0))
                     + (along_z - pltpu.roll(along_z, 1, 1)))
            hold[t] = along_x

    to_partner = {}

    def send_partner(x):
        to_partner[x] = start_copy(partial.at[x], arriving.at[x], me, None, partner)
        sends.append((to_partner[x], None))

    def emit_partner(x):
        def emit(t, value):
            partial[x, t] = value
        return emit

    def emit_own(x):
        def emit(t, value):
            at = pl.ds(own0 + x * rows, rows)
            b0[t, at, :] = source_ref[t, pl.ds(x * rows, rows), :] - value
        return emit

    def partner_step(now, later, hold, x, emits=True):
        advance(modes, KL, now, later, hold, x, emit_partner(x) if emits else None)

    merge = pairing()
    spread = spreading()
    own1 = PAD + 5 * r1
    size1 = n1 * r1
    own2 = PAD + 6 * r2
    size2 = n2 * r2
    columns = grid // 8
    all3 = columns * r3

    def gather_small(value, dest, turn):
        slots[turn, row_at, pl.ds(0, r3), :] = value
        copies = []
        for q in range(1, ROW):
            copy = start_copy(slots.at[turn, row_at], slots.at[turn, row_at], row_peer(q))
            sends.append((copy, None))
            copies.append((copy, None))

        def second():
            for pair in copies:
                arrived(pair)
            first = pl.multiple_of(PAD + col_at * (ROW * r3), 8)
            for n in range(0, ROW, 2):
                dest[pl.ds(first + n * r3, 2 * r3), :] = jnp.concatenate(
                    [slots[turn, n, pl.ds(0, r3), :], slots[turn, n + 1, pl.ds(0, r3), :]], axis=0)
            at = pl.ds(first, ROW * r3)
            more = []
            for q in range(1, cols):
                copy = start_copy(dest.at[at], dest.at[at], col_peer(q))
                sends.append((copy, None))
                more.append((copy, None))
            return more

        return second

    def coarse_coefficients():
        part = pair_xy(c0, own0, width, rows, temp)
        c1[pl.ds(own1, size1), :] = restrict_pair(part, part, merge)
        found = [
            to_neighbour(c1.at[pl.ds(own1, size1)], c1.at[pl.ds(own1 - size1, size1)], 1),
            to_neighbour(c1.at[pl.ds(own1, size1)], c1.at[pl.ds(own1 + size1, size1)], -1),
            to_neighbour(c1.at[pl.ds(own1 + size1 - r1, r1)], c1.at[pl.ds(own1 - size1 - r1, r1)], 2),
            to_neighbour(c1.at[pl.ds(own1, r1)], c1.at[pl.ds(own1 + 2 * size1, r1)], -2),
        ]
        part = pair_xy(c1, own1, n1, r1, temp)
        c2[pl.ds(own2, size2), :] = restrict_pair(part, part, merge)
        for delta in NEAR:
            found.append(to_neighbour(c2.at[pl.ds(own2, size2)], c2.at[pl.ds(own2 - delta * size2, size2)], delta))
        part = pair_xy(c2, own2, n2, r2, temp)
        return found, gather_small(restrict_pair(part, part, merge), c3, 0)

    def column_sums(values):
        gather = jnp.where(
            lax.broadcasted_iota(jnp.int32, (columns, all3), 1) // r3
            == lax.broadcasted_iota(jnp.int32, (columns, all3), 0), 1.0, 0.0)
        within = jnp.where(
            lax.broadcasted_iota(jnp.int32, (LANES, LANES), 1) // (LANES // 8)
            == lax.broadcasted_iota(jnp.int32, (LANES, LANES), 0) // (LANES // 8), 1.0, 0.0)
        return jnp.dot(
            jnp.dot(gather, values, precision=lax.Precision.HIGHEST, preferred_element_type=F32),
            within, precision=lax.Precision.HIGHEST, preferred_element_type=F32)

    def line_factors():
        diag3 = i3[pl.ds(PAD, all3), :]
        line[0] = column_sums(g3[1, pl.ds(PAD, all3), :] * diag3)
        line[2] = column_sums(g3[0, pl.ds(PAD, all3), :] * diag3)
        ratio = None
        for x in range(columns):
            low, high = line[0, pl.ds(x, 1), :], line[2, pl.ds(x, 1), :]
            den = low + high
            if ratio is not None:
                den = den - low * ratio
            inv = 1.0 / den
            ratio = high * inv
            line[0, pl.ds(x, 1), :] = low * inv
            line[1, pl.ds(x, 1), :] = inv
            line[2, pl.ds(x, 1), :] = ratio

    all_faces()
    pass_on(0)
    send_own(2)
    coarse_halos, coarse_second = coarse_coefficients()
    pass_on(1)
    send_own(3)
    complete(0)
    low = to_neighbour(q0, rim_low, 1)
    for ref in (s3, a3, d3):
        zero_all(ref)
    pass_on(2)
    send_own(4)
    complete(1)
    high = to_neighbour(q1, rim_high, -1)
    for ref in (s2, a2, d2, s1, a1, d1):
        zero_all(ref)
    pass_on(3)
    send_own(5)
    complete(2)
    arrived(low)
    fill(modes, KL, mix_a, -1)
    partner_step(mix_a, mix_b, hold_a, -1, False)
    partner_step(mix_b, mix_a, hold_a, 0)
    send_partner(0)
    pass_on(4)
    send_own(6)
    c3_more = coarse_second()
    complete(3)
    partner_step(mix_a, mix_b, hold_a, 1)
    send_partner(1)
    pass_on(5)
    send_own(7)
    for pair in coarse_halos:
        arrived(pair)
    level_faces(c1, g1, w1, i1, PAD + r1, (n1 + 8) * r1, 16, r1, LANES // 2, 0.25, me * n1 - 5, grid // 2)
    level_faces(c2, g2, w2, i2, PAD + r2, (n2 + 10) * r2, 16, r2, LANES // 4, 0.0625, me * n2 - 6, grid // 4)
    pass_on(6)
    complete(4)
    complete(5)
    arrived(high)
    fill(modes, KL, mix_c, 5)
    partner_step(mix_c, mix_d, hold_b, 5, False)
    partner_step(mix_d, mix_c, hold_b, 6)
    send_partner(6)
    pass_on(7)
    partner_step(mix_c, mix_d, hold_b, 7)
    send_partner(7)
    complete(6)
    partner_step(mix_b, mix_a, hold_a, 2)
    send_partner(2)
    complete(7)
    partner_step(mix_a, mix_b, hold_a, 3)
    partner_step(mix_b, mix_a, hold_a, 4)
    partner_step(mix_a, mix_b, hold_a, 5)
    send_partner(5)
    fill(0, KL + 1, mix_e, -1)
    now, later = mix_e, mix_f
    for x in range(-1, width):
        advance(0, KL + 1, now, later, hold_c, x, emit_own(x) if x >= 0 else None)
        now, later = later, now
        if x == 1:
            send_partner(3)
            send_partner(4)
    level_faces(c0, g0, w0, i0, PAD + rows, (width + 6) * rows, 16, rows, LANES, 1.0, me * width - 4, grid)
    for pair in c3_more:
        arrived(pair)
    level_faces(c3, g3, w3, i3, PAD, all3, 32, r3, LANES // 8, 0.015625, 0, grid // 8)
    line_factors()
    for ref in (s0, a0, d0):
        zero_all(ref)

    def receive(x):
        to_partner[x].wait_recv()
        at = pl.ds(own0 + x * rows, rows)
        for m in range(modes):
            value = b0[m, at, :] - arriving[x, m]
            b0[m, at, :] = value
            residual_ref[m, pl.ds(x * rows, rows), :] = value

    halos = []
    for x in (0, 1, 2):
        receive(x)
    halos.append(to_neighbour(b0.at[pl.ds(0, modes), pl.ds(own0, 3 * rows)], b0.at[pl.ds(0, modes), pl.ds(own0 + size0, 3 * rows)], -1))
    for x in (6, 7, 5):
        receive(x)
    halos.append(to_neighbour(b0.at[pl.ds(0, modes), pl.ds(own0 + size0 - 3 * rows, 3 * rows)], b0.at[pl.ds(0, modes), pl.ds(own0 - 3 * rows, 3 * rows)], 1))
    for x in (3, 4):
        receive(x)
    first_sweep(s0, b0, w0, modes, own0, size0, 32)
    sweep(a0, s0, s0, g0, modes, own0 + rows, size0 - 2 * rows, 64, rows)
    for pair in halos:
        arrived(pair)
    for at in (own0 - 3 * rows, own0 + size0):
        first_sweep(s0, b0, w0, modes, at, 3 * rows, 32)
    for at in (own0 - 2 * rows, own0 + size0 - rows):
        sweep(a0, s0, s0, g0, modes, at, 3 * rows, 32, rows)
    sweep(d0, a0, s0, g0, modes, own0, size0, 64, rows, inverse=i0)
    pairs1 = b1.shape[0]
    for p in range(pairs1):
        left = pair_xy(d0.at[2 * p], own0, width, rows, temp)
        right = pair_xy(d0.at[2 * p + 1], own0, width, rows, temp)
        b1[p, pl.ds(own1, size1), :] = restrict_pair(left, right, merge)
    b1_halos = [
        to_neighbour(b1.at[:, pl.ds(own1, size1)], b1.at[:, pl.ds(own1 - size1, size1)], 1),
        to_neighbour(b1.at[:, pl.ds(own1, size1)], b1.at[:, pl.ds(own1 + size1, size1)], -1),
    ]
    for pair in b1_halos:
        arrived(pair)
    first_sweep(s1, b1, w1, pairs1, PAD + r1, (n1 + 8) * r1, 32)
    sweep(a1, s1, s1, g1, pairs1, PAD + 2 * r1, (n1 + 6) * r1, 80, r1)
    sweep(d1, a1, s1, g1, pairs1, own1, size1, 64, r1, inverse=i1)
    pairs2 = b2.shape[0]
    for p in range(pairs2):
        left = pair_xy(d1.at[2 * p], own1, n1, r1, temp)
        right = pair_xy(d1.at[2 * p + 1], own1, n1, r1, temp)
        b2[p, pl.ds(own2, size2), :] = restrict_pair(left, right, merge)
    b2_halos = []
    for delta in NEAR:
        b2_halos.append(to_neighbour(b2.at[:, pl.ds(own2, size2)], b2.at[:, pl.ds(own2 - delta * size2, size2)], delta))
    for pair in b2_halos:
        arrived(pair)
    first_sweep(s2, b2, w2, pairs2, PAD + r2, (n2 + 10) * r2, 48)
    sweep(a2, s2, s2, g2, pairs2, PAD + 2 * r2, (n2 + 8) * r2, 40, r2)
    sweep(d2, a2, s2, g2, pairs2, own2, size2, 16, r2, inverse=i2)
    left = pair_xy(d2.at[0], own2, n2, r2, temp)
    right = pair_xy(d2.at[1], own2, n2, r2, temp)
    second = gather_small(restrict_pair(left, right, merge), b3.at[0], 1)
    for pair in second():
        arrived(pair)
    first_sweep(s3, b3, w3, 1, PAD, all3, all3)
    now, other = s3, a3
    for turn in range(COARSE - 1):
        sweep(other, now, s3, g3, 1, PAD, all3, all3, r3)
        now, other = (a3, d3) if now is s3 else (other, now)
    sweep(other, now, s3, g3, 1, PAD, all3, all3, r3, inverse=i3)
    sums[...] = column_sums(other[0, pl.ds(PAD, all3), :])
    carried = None
    for x in range(columns):
        value = sums[pl.ds(x, 1), :] * line[1, pl.ds(x, 1), :]
        if carried is not None:
            value = value + line[0, pl.ds(x, 1), :] * carried
        sums[pl.ds(x, 1), :] = value
        carried = value
    carried = None
    for x in reversed(range(columns)):
        value = sums[pl.ds(x, 1), :]
        if carried is not None:
            value = value + line[2, pl.ds(x, 1), :] * carried
        carried = value
        at = pl.ds(PAD + x * r3, r3)
        now[0, at, :] = now[0, at, :] + jnp.broadcast_to(value, (r3, LANES))
    for x in range(5):
        small[pl.ds(x * r3, r3), :] = now[0, pl.ds(PAD + (me + x - 2) * r3, r3), :]
    prolong(a2, pairs2, PAD + 2 * r2, lambda p: small[pl.ds(0, 5 * r3), :], 5, r3, spread, temp)
    sweep(d2, a2, s2, g2, pairs2, PAD + 3 * r2, (n2 + 6) * r2, 32, r2)
    sweep(a2, d2, s2, g2, pairs2, PAD + 4 * r2, (n2 + 4) * r2, 48, r2)
    prolong(a1, pairs1, PAD + r1, lambda p: a2[p, pl.ds(PAD + 4 * r2, (n2 + 4) * r2), :], n2 + 4, r2, spread, temp)
    sweep(d1, a1, s1, g1, pairs1, PAD + 3 * r1, (n1 + 4) * r1, 64, r1)
    sweep(a1, d1, s1, g1, pairs1, PAD + 4 * r1, (n1 + 2) * r1, 48, r1)
    prolong(a0, modes, PAD + 2 * rows, lambda p: a1[p, pl.ds(PAD + 4 * r1, (n1 + 2) * r1), :], n1 + 2, r1, spread, temp)
    sweep(d0, a0, s0, g0, modes, PAD + 3 * rows, (width + 2) * rows, 64, rows)
    sweep(a0, d0, s0, g0, modes, own0, size0, 64, rows)
    finish()


def coupling_places(coupling_list, mode, modes):
    side = mode % 2
    targets = jnp.concatenate([
        mode * modes + jnp.arange(modes, dtype=jnp.int32),
        (mode + 1 - 2 * side) * modes + jnp.arange(modes, dtype=jnp.int32),
    ])
    wanted = (targets[:, None] * 8 + jnp.arange(1, KL + 1, dtype=jnp.int32)[None, :]).reshape(-1)
    given = coupling_list[0] * 8 + coupling_list[2]
    other = coupling_list[1]
    held = (other // modes) % 2 == side
    slot = other // (2 * modes) * modes + other % modes
    match = jnp.logical_and(wanted[:, None] == given[None, :], held[None, :])
    code = jnp.where(match, slot * 4 + coupling_list[3], -1)
    high = jnp.max(code, axis=1)
    low = jnp.min(jnp.where(match, slot * 4 + coupling_list[3], 1 << 20), axis=1)
    low = jnp.where(low < high, low, 0)
    both = jnp.maximum(jnp.stack([high, low]), 0)
    return both // 4, jnp.sqrt((both % 4).astype(F32))


def local(blocks, pressure, source, kl_field, coupling_list):
    modes, width, rows, depth = pressure.shape
    plane = width * rows
    even = modes + modes % 2
    r1, r2, r3 = rows // 2, rows // 4, rows // 8
    grid = width * blocks
    n0 = (width + 8) * rows + 2 * PAD
    n1 = (width // 2 + 10) * r1 + 2 * PAD
    n2 = (width // 4 + 12) * r2 + 2 * PAD
    n3 = grid // 8 * r3 + 2 * PAD
    scratch = []
    for size, count in ((n0, even), (n1, even // 2), (n2, even // 4), (n3, 1)):
        scratch += [pltpu.VMEM((size, LANES), F32)] * 3
        scratch += [pltpu.VMEM((6, size, LANES), F32)]
        scratch += [pltpu.VMEM((count, size, LANES), F32)] * 4
    held = RING * modes
    scratch += [
        pltpu.VMEM((512, LANES), F32),
        pltpu.VMEM((3, grid // 8, LANES), F32),
        pltpu.VMEM((grid // 8, LANES), F32),
        pltpu.VMEM((24, LANES), F32),
        pltpu.VMEM((2, ROW, 8, LANES), F32),
    ]
    scratch += [pltpu.VMEM((held, count * rows, LANES), F32) for _, count in CHUNKS]
    scratch += [pltpu.VMEM((held, rows, LANES), F32)] * 2
    scratch += [pltpu.VMEM((KL, (width + 2) * rows + 2 * PAD, LANES), F32)]
    scratch += [pltpu.VMEM((KL + 1, (width + 1) * rows, LANES), F32)] * 3
    scratch += [pltpu.VMEM((modes * KL, rows + 8, LANES), F32)] * 4
    scratch += [pltpu.VMEM((modes * (KL + 1), rows + 8, LANES), F32)] * 2
    scratch += [pltpu.VMEM((modes, rows, LANES), F32)] * 3
    scratch += [pltpu.VMEM((width, modes, rows, LANES), F32)] * 2
    scratch += [pltpu.SemaphoreType.DMA((COPIES,))] * 2
    geometry = (modes, width, rows, blocks)
    places, shares = coupling_places(coupling_list, lax.axis_index("mode"), modes)
    shape = jax.ShapeDtypeStruct((modes, plane, depth), F32)
    out, residual = pl.pallas_call(
        lambda *refs: cycle_kernel(geometry, *refs),
        out_shape=(shape, shape),
        in_specs=[pl.BlockSpec(memory_space=pltpu.SMEM)] * 2 + [pl.BlockSpec(memory_space=pltpu.VMEM)] * 3,
        out_specs=[pl.BlockSpec(memory_space=pltpu.VMEM)] * 2,
        scratch_shapes=scratch,
        compiler_params=pltpu.CompilerParams(
            collective_id=1, has_side_effects=True, vmem_limit_bytes=60 * 2**20),
        name="coupled_cycle",
    )(places, shares, pressure.reshape(modes, plane, depth), source.reshape(modes, plane, depth),
      kl_field.reshape(KL + 1, plane, depth))
    return (out.reshape(pressure.shape), residual.reshape(pressure.shape))


def solution(mesh):
    in_specs = (
        P("mode", "space", None, None),
        P("mode", "space", None, None),
        P(None, "space", None, None),
        P(),
    )
    out_specs = (P("mode", "space", None, None), P("mode", "space", None, None))
    blocks = mesh.shape["space"]
    return jax.shard_map(lambda *arrays: local(blocks, *arrays), mesh=mesh, in_specs=in_specs, out_specs=out_specs, check_vma=False)
```
